32 devices in a mesh: branch: 4 (over x, core), query: 8 (over z, y).
Axes of the slice: x: 2, y: 2, z: 4, core: 2. Of those that a mesh axis runs over, the one named last changes fastest.
Arguments:
- sensors: bfloat16 [3, 32, 2048], P(None, ('branch', 'query')), may hold values from -6 to 6
- branch_w: bfloat16 [3, 2048, 1024], replicated, may hold values from -0.125 to 0.125
- branch_b: float32 [3, 1024], replicated, may hold values from -3 to 3
- coords: bfloat16 [3, 16384], P(None, ('branch', 'query')), may hold values from -1 to 1
- func_index: int32 [16384], P(('branch', 'query')), may hold values from 0 to 7
- targets: float32 [16384], P(('branch', 'query')), may hold values from -6 to 6
- trunk_w1: bfloat16 [3, 1024], replicated, may hold values from -3.5 to 3.5
- trunk_b1: float32 [1024], replicated, may hold values from -3 to 3
- trunk_w2: bfloat16 [1024, 1024], replicated, may hold values from -0.1875 to 0.1875
- trunk_b2: float32 [1024], replicated, may hold values from -3 to 3
Outputs:
- grad_branch_w: float32 [3, 2048, 1024], P(None, 'query')
- grad_branch_b: float32 [3, 1024], replicated
- grad_trunk_w1: float32 [3, 1024], replicated
- grad_trunk_b1: float32 [1024], replicated
- grad_trunk_w2: float32 [1024, 1024], replicated
- grad_trunk_b2: float32 [1024], replicated
The draws below stay inside these ranges and needn't reach their ends.
Inputs may be any that keep to these rules, and one draw needn't show every extreme that they name: func_index[i] names one of the 8 function samples whose rows of sensors stand in the same owner group (index of the mesh axis branch) as query point i.
All inputs are finite; a program needn't handle non-finite values.
Results may differ from the reference program's by a relative error of at most 0.018.
Values may be sent and summed in bfloat16 or wider, within the bound.
No kernel may reach another device: no remote copies, remote signals or barrier semaphores. Data moves between devices by JAX's collectives and lax.ppermute only.
A program may use at most 128 MiB of HBM per device.

```python
import jax
import jax.numpy as jnp
from jax import lax

BRANCHES = 3
DIMS = 3
SENSORS = 2048
LATENT = 1024
HIDDEN_SIZE = 1024
QRY_DEV = 512
GROUP_FUNCS = 8
FUNCS = 32
QUERIES = 16384
N_QUERY = 8


def with_ends(result, key, least, largest):
    extent = result.shape
    index_at = [jax.random.randint(jax.random.fold_in(key, axis), (), 0, extent[axis]) for axis in range(len(extent))]
    result = result.at[tuple(index_at)].set(least)
    longest = extent.index(max(extent))
    index_at[longest] = (index_at[longest] + 1) % extent[longest]
    return result.at[tuple(index_at)].set(largest)


def spiked(entries, rng, source, target, shards_of, factor):
    def block_of(axis_at):
        return (jnp.arange(entries.shape[axis_at]) // (entries.shape[axis_at] // shards_of)).reshape((-1,) + (1,) * (entries.ndim - 1 - axis_at))

    one_side = jax.random.permutation(rng, shards_of)[block_of(target)]
    second = (block_of(target) + shards_of // 2) % shards_of
    return jnp.where((block_of(source) == one_side) | (block_of(source) == second), factor * entries, entries)


def steps_of(key, shape, shards, low, high):
    level = 1.0
    for axis_at, parts in shards:
        draws = jax.random.uniform(jax.random.fold_in(jax.random.fold_in(key, 6), axis_at), (parts,), jnp.float32, low / len(shards), high / len(shards))
        level = level * jnp.repeat(jnp.exp(draws), shape[axis_at] // parts).reshape((-1,) + (1,) * (len(shape) - 1 - axis_at))
    return level


def bell_draw(key, shape, width, most, pieces=(), held_as=jnp.bfloat16):
    gain = steps_of(key, shape, pieces, -0.22, 0.18) if pieces else 1.0
    array = jax.random.normal(key, shape, jnp.float32) * width * gain
    return jnp.minimum(jnp.maximum(array, -most), most).astype(held_as)


def gaussian_with(key, extent, spread, most, split, heavy, kind=jnp.bfloat16):
    entries = spread * jax.random.normal(key, extent, jnp.float32)
    if split:
        entries = entries * steps_of(key, extent, split, -0.22, 0.18)
    return jnp.clip(spiked(entries, jax.random.fold_in(key, 3), *heavy), -most, most).astype(kind)


def setup_inputs(seed: int = 0) -> dict:
    splits = jax.random.split(jax.random.key(seed), 11)
    return {
        "sensors": gaussian_with(splits[0], (BRANCHES, FUNCS, SENSORS), 1.0, 6.0, ((1, 32),), (1, 2, 32, 2.75)),
        "branch_w": bell_draw(splits[1], (BRANCHES, SENSORS, LATENT), SENSORS ** -0.5, 0.125),
        "branch_b": bell_draw(splits[2], (BRANCHES, LATENT), 0.5, 3.0, (), jnp.float32),
        "coords": jnp.clip(jax.random.uniform(splits[3], (DIMS, QUERIES), jnp.float32, -1.0, 1.0) * steps_of(splits[3], (DIMS, QUERIES), ((1, 32),), -0.4, 0.0), -1.0, 1.0).astype(jnp.bfloat16),
        "func_index": with_ends(jax.random.randint(splits[4], (QUERIES,), 0, GROUP_FUNCS), jax.random.fold_in(splits[4], 1), 0, GROUP_FUNCS - 1).astype(jnp.int32),
        "targets": bell_draw(splits[5], (QUERIES,), 1.0, 6.0, ((0, 32),), jnp.float32),
        "trunk_w1": bell_draw(splits[6], (DIMS, HIDDEN_SIZE), DIMS ** -0.5, 3.5),
        "trunk_b1": bell_draw(splits[7], (HIDDEN_SIZE,), 0.5, 3.0, (), jnp.float32),
        "trunk_w2": bell_draw(splits[8], (HIDDEN_SIZE, LATENT), HIDDEN_SIZE ** -0.5, 0.1875),
        "trunk_b2": bell_draw(splits[9], (LATENT,), 0.5, 3.0, (), jnp.float32),
    }


def reference(sensors, branch_w, branch_b, coords, func_index, targets, trunk_w1, trunk_b1, trunk_w2, trunk_b2):
    pre = jnp.einsum('kfs,ksl->kfl', sensors.astype(jnp.float32), branch_w.astype(jnp.float32)) + branch_b[:, None, :]
    latent = jnp.tanh(pre).astype(jnp.bfloat16)
    lat_full = latent.astype(jnp.float32)
    product = (lat_full[0] * lat_full[1] * lat_full[2]).astype(jnp.bfloat16)
    prod_full = product.astype(jnp.float32)
    scale = LATENT ** -0.5
    blocks = QUERIES // QRY_DEV
    coord_blocks = coords.reshape(DIMS, blocks, QRY_DEV).transpose(1, 0, 2)
    index_blocks = func_index.reshape(blocks, QRY_DEV)
    target_blocks = targets.reshape(blocks, QRY_DEV)

    def visit(carry, item):
        gw1, gb1, gw2, gb2, dprod = carry
        number, cblock, iblock, tblock = item
        owner = (iblock + (number // N_QUERY) * GROUP_FUNCS).astype(jnp.int32)
        first = lax.dot_general(cblock, trunk_w1, (((0,), (0,)), ((), ())), preferred_element_type=jnp.float32)
        hidden = jnp.tanh(first + trunk_b1).astype(jnp.bfloat16)
        trunk_out = jnp.dot(hidden, trunk_w2, preferred_element_type=jnp.float32) + trunk_b2
        picked = jnp.take(prod_full, owner, axis=0)
        pred = jnp.sum(picked * trunk_out, axis=1) * scale
        resid = (pred - tblock) / FUNCS
        weighted = (resid[:, None] * trunk_out * scale).astype(jnp.bfloat16)
        dprod = dprod + jax.ops.segment_sum(weighted.astype(jnp.float32), owner, FUNCS)
        grad_out = (resid[:, None] * picked * scale).astype(jnp.bfloat16)
        gw2 = gw2 + lax.dot_general(hidden, grad_out, (((0,), (0,)), ((), ())), preferred_element_type=jnp.float32)
        gb2 = gb2 + jnp.sum(grad_out.astype(jnp.float32), axis=0)
        grad_hidden = lax.dot_general(grad_out, trunk_w2, (((1,), (1,)), ((), ())), preferred_element_type=jnp.float32)
        hid_full = hidden.astype(jnp.float32)
        grad_pre = (grad_hidden * (1.0 - hid_full * hid_full)).astype(jnp.bfloat16)
        gw1 = gw1 + lax.dot_general(cblock, grad_pre, (((1,), (0,)), ((), ())), preferred_element_type=jnp.float32)
        gb1 = gb1 + jnp.sum(grad_pre.astype(jnp.float32), axis=0)
        return (gw1, gb1, gw2, gb2, dprod), None

    start = (jnp.zeros((DIMS, HIDDEN_SIZE), jnp.float32), jnp.zeros((HIDDEN_SIZE,), jnp.float32),
             jnp.zeros((HIDDEN_SIZE, LATENT), jnp.float32), jnp.zeros((LATENT,), jnp.float32),
             jnp.zeros((FUNCS, LATENT), jnp.float32))
    numbers = jnp.arange(blocks, dtype=jnp.int32)
    (gw1, gb1, gw2, gb2, dprod), _ = lax.scan(visit, start, (numbers, coord_blocks, index_blocks, target_blocks))
    others = jnp.stack([lat_full[1] * lat_full[2], lat_full[0] * lat_full[2], lat_full[0] * lat_full[1]])
    delta = (dprod[None] * others * (1.0 - lat_full * lat_full)).astype(jnp.bfloat16)
    delta_full = delta.astype(jnp.float32)
    grad_branch_w = jnp.einsum('kfs,kfl->ksl', sensors.astype(jnp.float32), delta_full)
    grad_branch_b = jnp.sum(delta_full, axis=1)
    return grad_branch_w, grad_branch_b, gw1, gb1, gw2, gb2
```

```python
import jax
import jax.numpy as jnp
from jax import lax
from jax.sharding import PartitionSpec as P

BF = jnp.bfloat16
F32 = jnp.float32


def pieces(value, count):
    out = []
    for _ in range(count):
        top = lax.reduce_precision(value, 8, 7)
        out.append(top.astype(BF))
        value = value - top
    return out


def dot(a, b, dims):
    return lax.dot_general(a, b, (dims, ((), ())), preferred_element_type=F32)


def shards(
    sensors, branch_w, branch_b, coords, func_index, targets, trunk_w1, trunk_b1, trunk_w2, trunk_b2
):
    branches, func_dev, sensor_count = sensors.shape
    dims, queries = coords.shape
    width = branch_w.shape[2]
    scale = width ** (-0.5)
    nb, nq = lax.axis_size("branch"), lax.axis_size("query")
    total_funcs = func_dev * nb * nq
    group_funcs = func_dev * nq

    parts = [sensors.reshape(-1, queries), coords, func_index.astype(BF)[None]]
    parts += [t[None] for t in pieces(targets, 3)]
    packed = jnp.concatenate(parts, axis=0)
    rows = packed.shape[0]
    packed = jnp.pad(packed, ((0, -rows % 8), (0, 0)))
    sent = jnp.broadcast_to(packed[None], (nq,) + packed.shape)
    got = lax.all_to_all(sent, "query", 0, 0, tiled=True)
    first = rows - dims - 4
    group_sensors = (
        got[:, :first]
        .reshape(nq, branches, func_dev, sensor_count)
        .transpose(1, 0, 2, 3)
        .reshape(branches, group_funcs, sensor_count)
    )
    tail = got[:, first:rows].transpose(1, 0, 2).reshape(dims + 4, nq * queries)
    q_coords = tail[:dims]
    q_index = tail[dims].astype(jnp.int32)
    q_target = tail[dims + 1].astype(F32) + tail[dims + 2].astype(F32) + tail[dims + 3].astype(F32)

    pre = (
        jnp.einsum("kfs,ksl->kfl", group_sensors, branch_w, preferred_element_type=F32)
        + branch_b[:, None, :]
    )
    latent = jnp.tanh(pre).astype(BF)
    lat = latent.astype(F32)
    product = (lat[0] * lat[1] * lat[2]).astype(BF)

    mixed = dot(product, trunk_w2, ((1,), (1,)))
    offset = jnp.sum(product.astype(F32) * trunk_b2, axis=1, keepdims=True)
    first = dot(trunk_w1, q_coords, ((0,), (0,)))
    hidden = jnp.tanh(first + trunk_b1[:, None]).astype(BF)
    hi, lo = pieces(mixed, 2)
    scores = dot(jnp.concatenate([hi, lo], 0), hidden, ((1,), (0,)))
    scores = scores[:group_funcs] + scores[group_funcs:] + offset
    owned = (q_index[None, :] == jnp.arange(group_funcs, dtype=jnp.int32)[:, None]).astype(F32)
    pred = jnp.sum(owned * scores, axis=0) * scale
    resid = (pred - q_target) / total_funcs
    coef = owned * (resid * scale)[None]
    weights = jnp.concatenate(pieces(coef, 2), 0)
    g = dot(weights, hidden, ((1,), (1,)))
    g = (g[:group_funcs] + g[group_funcs:]).astype(BF)
    r = jnp.sum(coef, axis=1)
    hid = hidden.astype(F32)
    slope = (1.0 - hid * hid).astype(BF)
    ones = jnp.concatenate([jnp.ones_like(q_coords[:1]), q_coords], 0).astype(F32)
    spread = (ones[:, None] * coef[None]).reshape((dims + 1) * group_funcs, -1)
    moments = dot(jnp.concatenate(pieces(spread, 2), 0), slope, ((1,), (1,)))
    moments = moments.reshape(2, dims + 1, group_funcs, -1).sum(0)
    first_grads = jnp.sum(moments * mixed[None], axis=1)

    begin = lax.axis_index("query") * (sensor_count // nq)
    cut = lax.dynamic_slice_in_dim(group_sensors, begin, sensor_count // nq, 2)

    def gather(x):
        index = [[(i, (i + k) % nb) for i in range(nb)] for k in range(1, nb)]
        return [x] + [lax.ppermute(x, "branch", pairs) for pairs in index]

    r_row = jnp.pad(jnp.concatenate(pieces(r, 2)), (0, width - 2 * group_funcs))
    late = jnp.concatenate([g, first_grads.astype(BF), r_row[None]], 0)
    early = jnp.concatenate([latent.reshape(-1, width), cut.reshape(-1, width)], 0)
    earlies, lates = gather(early), gather(late)
    lat_rows = branches * group_funcs
    latent = jnp.concatenate(
        [e[:lat_rows].reshape(branches, group_funcs, width) for e in earlies], 1
    )
    cut = jnp.concatenate([e[lat_rows:].reshape(cut.shape) for e in earlies], 1)
    g = jnp.concatenate([x[:group_funcs] for x in lates], 0)
    first_grads = sum(x[group_funcs : group_funcs + dims + 1].astype(F32) for x in lates)
    r_rows = jnp.stack([x[-1].astype(F32) for x in lates])
    r = (r_rows[:, :group_funcs] + r_rows[:, group_funcs : 2 * group_funcs]).reshape(-1)

    lat = latent.astype(F32)
    product = (lat[0] * lat[1] * lat[2]).astype(BF)
    gw2 = dot(g, product, ((0,), (0,)))
    gb2 = jnp.sum(r[:, None] * product.astype(F32), axis=0)
    dprod = dot(g, trunk_w2, ((1,), (0,))) + r[:, None] * trunk_b2
    others = jnp.stack([lat[1] * lat[2], lat[0] * lat[2], lat[0] * lat[1]])
    delta = (dprod[None] * others * (1.0 - lat * lat)).astype(BF)
    gbw = jnp.einsum("kfs,kfl->ksl", cut, delta, preferred_element_type=F32)
    gbb = jnp.sum(delta.astype(F32), axis=1)
    return (gbw, gbb, first_grads[1:], first_grads[0], gw2, gb2)


def solution(mesh):
    placed = (
        P(None, ("branch", "query"), None),
        P(),
        P(),
        P(None, ("branch", "query")),
        P(("branch", "query")),
        P(("branch", "query")),
        P(),
        P(),
        P(),
        P(),
    )
    return jax.shard_map(
        shards,
        mesh=mesh,
        in_specs=placed,
        out_specs=(P(None, "query", None), P(), P(), P(), P(), P()),
        check_vma=False,
    )
```

```python
import functools

import jax
import jax.numpy as jnp
from jax import lax
from jax.experimental import pallas as pl
from jax.experimental.pallas import tpu as pltpu
from jax.sharding import PartitionSpec as P

BF = jnp.bfloat16
F32 = jnp.float32
MIB = 1 << 20
VMEM = pl.BlockSpec(memory_space=pltpu.VMEM)
ANY = pl.BlockSpec(memory_space=pl.ANY)


def up(value, step):
    return -(-value // step) * step


def pieces(value, count):
    out = []
    for _ in range(count):
        top = value.astype(BF)
        out.append(top)
        value = value - top.astype(F32)
    return out


def dot(a, b, dims=((1,), (0,))):
    return lax.dot_general(a, b, (dims, ((), ())), preferred_element_type=F32)


def stack(rows, count):
    have = sum(r.shape[0] for r in rows)
    if have < count:
        rows = rows + [jnp.zeros((count - have, rows[0].shape[1]), rows[0].dtype)]
    return jnp.concatenate(rows, axis=0)


def pack_kernel(sensors_ref, coords_ref, index_ref, targets_ref, out_ref):
    peers, rows, q = out_ref.shape
    branches, sensor_count = sensors_ref.shape
    cut = sensor_count // peers
    s = sensors_ref[...].astype(F32)
    base = [s[k : k + 1, c : c + q] for k in range(branches) for c in range(0, sensor_count, q)]
    base += [coords_ref[...].astype(F32), index_ref[...].astype(F32)]
    base += [t.astype(F32) for t in pieces(targets_ref[...], 3)]
    have = sum(r.shape[0] for r in base)
    whole = have // 8 * 8
    both = jnp.concatenate(base, axis=0)
    top, rest = both[:whole], both[whole:]
    flat = up(branches * cut, q)
    for j in range(peers):
        line = [s[k : k + 1, j * cut : (j + 1) * cut] for k in range(branches)]
        if flat > branches * cut:
            line.append(jnp.zeros((1, flat - branches * cut), F32))
        line = jnp.concatenate(line, axis=1)
        tail = [rest] + [line[:, c : c + q] for c in range(0, flat, q)]
        out_ref[j] = jnp.concatenate([top, stack(tail, rows - whole)], axis=0).astype(BF)


def latent_kernel(cut_row, got_ref, w_ref, bias_ref, w2_ref, b2_ref, early_ref, mixed_ref, offset_ref):
    _, funcs, q = got_ref.shape
    branches, sensor_count, width = w_ref.shape
    per = sensor_count // q
    lats = []
    for k in range(branches):
        x = jnp.concatenate([got_ref[k * per + c] for c in range(per)], axis=1)
        pre = dot(x, w_ref[k]) + bias_ref[k : k + 1, :]
        lats.append(jnp.tanh(pre).astype(BF).astype(F32))
    product = (lats[0] * lats[1] * lats[2]).astype(BF)
    lines = [got_ref[cut_row + c].astype(F32) for c in range(up(branches * sensor_count // funcs, q) // q)]
    if len(lines) * q < width:
        lines.append(jnp.zeros((funcs, width - len(lines) * q), F32))
    early_ref[...] = jnp.concatenate(lats + [jnp.concatenate(lines, axis=1)], axis=0).astype(BF)
    mixed_ref[...] = dot(product, w2_ref[...], ((1,), (1,)))
    offset = jnp.sum(product.astype(F32) * b2_ref[...], axis=1, keepdims=True)
    offset_ref[...] = jnp.broadcast_to(offset, offset_ref.shape)


def trunk_kernel(
    row, dims, total_funcs, unroll,
    got_ref, mixed_ref, offset_ref, w1_ref, b1_ref, late_ref, h_ref, s_ref, g_ref, m_ref, r_ref,
):
    chunks, _, q = got_ref.shape
    funcs, width = mixed_ref.shape
    scale = width ** (-0.5)
    known = up(dims + 3, 8)
    first = stack([w1_ref[...].astype(F32)] + [b.astype(F32) for b in pieces(b1_ref[...], 3)], known)
    first = first.astype(BF)
    mixed = jnp.concatenate(pieces(mixed_ref[...], 2), axis=0)
    offset = offset_ref[:, 0:1]
    lane_of = lax.broadcasted_iota(jnp.int32, (funcs, q), 0).astype(F32)
    g_ref[...] = jnp.zeros_like(g_ref)
    m_ref[...] = jnp.zeros_like(m_ref)
    r_ref[...] = jnp.zeros_like(r_ref)

    def visit(j, slot):
        block = got_ref[j].astype(F32)
        xyz = block[row : row + dims]
        owner = block[row + dims : row + dims + 1]
        target = block[row + dims + 1 : row + dims + 2]
        target = target + block[row + dims + 2 : row + dims + 3]
        target = target + block[row + dims + 3 : row + dims + 4]
        a = stack([xyz, jnp.ones((3, q), F32)], known).T.astype(BF)
        h = jnp.tanh(dot(a, first)).astype(BF)
        h_ref[slot] = h
        hf = h.astype(F32)
        s_ref[slot] = (1.0 - hf * hf).astype(BF)
        scores = dot(mixed, h_ref[slot], ((1,), (1,)))
        scores = scores[:funcs] + scores[funcs:] + offset
        owned = (owner == lane_of).astype(F32)
        pred = jnp.sum(owned * scores, axis=0, keepdims=True) * scale
        resid = (pred - target) / total_funcs
        coef = owned * (resid * scale)
        g_ref[...] += dot(jnp.concatenate(pieces(coef, 2), axis=0), h_ref[slot])
        spread = jnp.concatenate([coef] + [coef * xyz[d : d + 1] for d in range(dims)], axis=0)
        m_ref[...] += dot(jnp.concatenate(pieces(spread, 2), axis=0), s_ref[slot])
        r_ref[...] += coef

    if chunks == unroll:
        for j in range(chunks):
            visit(j, j)
    else:
        def several(i, carry):
            for u in range(unroll):
                visit(i * unroll + u, u)
            return carry
        lax.fori_loop(0, chunks // unroll, several, 0)

    g = g_ref[:funcs] + g_ref[funcs:]
    r = jnp.broadcast_to(jnp.sum(r_ref[...], axis=1, keepdims=True), (funcs, late_ref.shape[1] - width))
    high, low = pieces(r, 2)
    lane = lax.broadcasted_iota(jnp.int32, r.shape, 1)
    r = jnp.where(lane < r.shape[1] // 2, high.astype(F32), low.astype(F32))
    half = (dims + 1) * funcs
    moments = m_ref[:half] + m_ref[half:]
    grads = [
        jnp.sum(moments[d * funcs : (d + 1) * funcs] * mixed_ref[...], axis=0, keepdims=True)
        for d in range(dims + 1)
    ]
    grads = jnp.concatenate(grads, axis=0)
    grads = jnp.concatenate([grads, jnp.zeros((dims + 1, r.shape[1]), F32)], axis=1)
    late_ref[...] = stack([jnp.concatenate([g, r], axis=1), grads], late_ref.shape[0]).astype(BF)


def tail_kernel(
    groups, funcs, dims, cut,
    *refs,
):
    earlies, lates = refs[:groups], refs[groups : 2 * groups]
    w2_ref, b2_ref, gbw_ref, gbb_ref, gw1_ref, gb1_ref, gw2_ref, gb2_ref, gbw_buf, gw2_buf, sems = refs[2 * groups :]
    width = w2_ref.shape[1]
    branches = gbw_ref.shape[0]
    early = [e[...].astype(F32) for e in earlies]
    late = [x[...].astype(F32) for x in lates]

    def rows(parts, first):
        return jnp.concatenate([p[first : first + funcs] for p in parts], axis=0)

    lat = [rows(early, k * funcs) for k in range(branches)]
    lines = rows(early, branches * funcs)
    product = (lat[0] * lat[1] * lat[2]).astype(BF)
    ends = rows(late, 0)
    g, r = ends[:, :width], ends[:, width:]
    r = r[:, :1] + r[:, r.shape[1] // 2 : r.shape[1] // 2 + 1]
    copies = []

    def send(buf, out, index):
        copy = pltpu.make_async_copy(buf, out, sems.at[index])
        copy.start()
        copies.append(copy)

    height = gw2_buf.shape[1]
    for c in range(gw2_buf.shape[0]):
        gw2_buf[c] = dot(g[:, c * height : (c + 1) * height].T.astype(BF), product)
        send(gw2_buf.at[c], gw2_ref.at[pl.ds(c * height, height)], c)
    dprod = dot(g.astype(BF), w2_ref[...]) + r * b2_ref[...]
    gbb = []
    for k in range(branches):
        others = [lat[j] for j in range(branches) if j != k]
        delta = (dprod * (others[0] * others[1]) * (1.0 - lat[k] * lat[k])).astype(BF)
        gbw_buf[k] = dot(lines[:, k * cut : (k + 1) * cut].T.astype(BF), delta)
        send(gbw_buf.at[k], gbw_ref.at[k], gw2_buf.shape[0] + k)
        gbb.append(jnp.sum(delta.astype(F32), axis=0, keepdims=True))
    gbb_ref[...] = jnp.concatenate(gbb, axis=0)
    grads = late[0][funcs : funcs + dims + 1, :width]
    for x in late[1:]:
        grads = grads + x[funcs : funcs + dims + 1, :width]
    gb1_ref[...] = grads[:1]
    gw1_ref[...] = grads[1:]
    gb2_ref[...] = jnp.sum(r * product.astype(F32), axis=0, keepdims=True)
    for copy in copies:
        copy.wait()


def shards(
    sensors, branch_w, branch_b, coords, func_index, targets, trunk_w1, trunk_b1, trunk_w2, trunk_b2
):
    branches, func_dev, sensor_count = sensors.shape
    dims, queries = coords.shape
    hidden, width = trunk_w2.shape
    nb, nq = lax.axis_size("branch"), lax.axis_size("query")
    assert func_dev == 1 and sensor_count % queries == 0 and hidden == width
    funcs = nq
    cut = sensor_count // nq
    row = branches * sensor_count // queries
    cut_row = row + dims + 4
    rows = up(cut_row + up(branches * cut, queries) // queries, 8)

    packed = pl.pallas_call(
        pack_kernel,
        out_shape=jax.ShapeDtypeStruct((nq, rows, queries), BF),
        in_specs=[VMEM] * 4,
        out_specs=VMEM,
        compiler_params=pltpu.CompilerParams(vmem_limit_bytes=8 * MIB),
        name="pack",
    )(sensors.reshape(branches, sensor_count), coords, func_index[None], targets[None])
    got = lax.all_to_all(packed, "query", 0, 0, tiled=True)

    early, mixed, offset = pl.pallas_call(
        functools.partial(latent_kernel, cut_row),
        out_shape=(
            jax.ShapeDtypeStruct(((branches + 1) * funcs, width), BF),
            jax.ShapeDtypeStruct((funcs, hidden), F32),
            jax.ShapeDtypeStruct((funcs, 128), F32),
        ),
        in_specs=[VMEM] * 5,
        out_specs=(VMEM,) * 3,
        compiler_params=pltpu.CompilerParams(vmem_limit_bytes=24 * MIB),
        cost_estimate=pl.CostEstimate(
            flops=2 * funcs * branch_w.size, bytes_accessed=2 * branch_w.size, transcendentals=0
        ),
        name="latents",
    )(got.transpose(1, 0, 2), branch_w, branch_b, trunk_w2, trunk_b2[None])

    unroll = min(nq, 8)
    late_rows = up(funcs + dims + 1, 16)
    late = pl.pallas_call(
        functools.partial(trunk_kernel, row, dims, nb * nq, unroll),
        out_shape=jax.ShapeDtypeStruct((late_rows, width + 128), BF),
        in_specs=[VMEM] * 5,
        out_specs=VMEM,
        scratch_shapes=[
            pltpu.VMEM((unroll, queries, hidden), BF),
            pltpu.VMEM((unroll, queries, hidden), BF),
            pltpu.VMEM((2 * funcs, hidden), F32),
            pltpu.VMEM((2 * (dims + 1) * funcs, hidden), F32),
            pltpu.VMEM((funcs, queries), F32),
        ],
        compiler_params=pltpu.CompilerParams(vmem_limit_bytes=32 * MIB),
        cost_estimate=pl.CostEstimate(
            flops=2 * 1024 * nq * queries * hidden, bytes_accessed=2 * MIB, transcendentals=nq * queries * hidden
        ),
        name="trunk",
    )(got, mixed, offset, trunk_w1, trunk_b1[None])

    def gather(x):
        shifts = [[(i, (i + k) % nb) for i in range(nb)] for k in range(1, nb)]
        return [x] + [lax.ppermute(x, "branch", pairs) for pairs in shifts]

    earlies, lates = gather(early), gather(late)
    blocks = 4
    gbw, gbb, gw1, gb1, gw2, gb2 = pl.pallas_call(
        functools.partial(tail_kernel, nb, funcs, dims, cut),
        out_shape=(
            jax.ShapeDtypeStruct((branches, cut, width), F32),
            jax.ShapeDtypeStruct((branches, width), F32),
            jax.ShapeDtypeStruct((dims, hidden), F32),
            jax.ShapeDtypeStruct((1, hidden), F32),
            jax.ShapeDtypeStruct((hidden, width), F32),
            jax.ShapeDtypeStruct((1, width), F32),
        ),
        in_specs=[VMEM] * (2 * nb + 2),
        out_specs=(ANY, VMEM, VMEM, VMEM, ANY, VMEM),
        scratch_shapes=[
            pltpu.VMEM((branches, cut, width), F32),
            pltpu.VMEM((blocks, hidden // blocks, width), F32),
            pltpu.SemaphoreType.DMA((blocks + branches,)),
        ],
        compiler_params=pltpu.CompilerParams(vmem_limit_bytes=24 * MIB),
        name="tail",
    )(*earlies, *lates, trunk_w2, trunk_b2[None])
    return (gbw, gbb, gw1, gb1[0], gw2, gb2[0])


def solution(mesh):
    placed = (
        P(None, ("branch", "query"), None),
        P(),
        P(),
        P(None, ("branch", "query")),
        P(("branch", "query")),
        P(("branch", "query")),
        P(),
        P(),
        P(),
        P(),
    )
    return jax.shard_map(
        shards,
        mesh=mesh,
        in_specs=placed,
        out_specs=(P(None, "query", None), P(), P(), P(), P(), P()),
        check_vma=False,
    )
```

```python
import functools

import jax
import jax.numpy as jnp
from jax import lax
from jax.experimental import pallas as pl
from jax.experimental.pallas import tpu as pltpu
from jax.sharding import PartitionSpec as P

BF = jnp.bfloat16
F32 = jnp.float32
MIB = 1 << 20
VMEM = pl.BlockSpec(memory_space=pltpu.VMEM)
HBM = pl.BlockSpec(memory_space=pltpu.HBM)


def up(value, step):
    return -(-value // step) * step


def pieces(value, count):
    out = []
    for _ in range(count):
        top = value.astype(BF)
        out.append(top)
        value = value - top.astype(F32)
    return out


def dot(a, b, dims=((1,), (0,))):
    return lax.dot_general(a, b, (dims, ((), ())), preferred_element_type=F32)


def stack(rows, count):
    have = sum(r.shape[0] for r in rows)
    if have < count:
        rows = rows + [jnp.zeros((count - have, rows[0].shape[1]), rows[0].dtype)]
    return jnp.concatenate(rows, axis=0)


def in_hbm(*arrays):
    return [pltpu.with_memory_space_constraint(a, pltpu.HBM) for a in arrays]


def first_layer(w1_ref, b1_ref):
    rows = [w1_ref[...].astype(F32)] + [b.astype(F32) for b in pieces(b1_ref[...], 3)]
    return stack(rows, up(w1_ref.shape[0] + 3, 8)).astype(BF)


def hidden_units(xyz, first):
    a = stack([xyz, jnp.ones((3, xyz.shape[1]), F32)], first.shape[0]).T.astype(BF)
    return jnp.tanh(dot(a, first)).astype(BF)


def for_chunks(chunks, unroll, visit):
    if chunks == unroll:
        for j in range(chunks):
            visit(j, j)
    else:
        def several(i, carry):
            for u in range(unroll):
                visit(i * unroll + u, u)
            return carry
        lax.fori_loop(0, chunks // unroll, several, 0)


def fetch(sems, first, *pairs):
    copies = [pltpu.make_async_copy(src, dst, sems.at[first + i]) for i, (src, dst) in enumerate(pairs)]
    for copy in copies:
        copy.start()
    return copies


def wait(copies):
    for copy in copies:
        copy.wait()


def pack_kernel(sensors_hbm, coords_hbm, index_hbm, targets_hbm, out_ref, sensors_ref, coords_ref, index_ref, targets_ref, sems):
    wait(fetch(
        sems, 0, (sensors_hbm, sensors_ref), (coords_hbm, coords_ref), (index_hbm, index_ref), (targets_hbm, targets_ref)
    ))
    peers, rows, q = out_ref.shape
    branches, sensor_count = sensors_ref.shape
    cut = sensor_count // peers
    s = sensors_ref[...].astype(F32)
    base = [s[k : k + 1, c : c + q] for k in range(branches) for c in range(0, sensor_count, q)]
    base += [coords_ref[...].astype(F32), index_ref[...].astype(F32)]
    base += [t.astype(F32) for t in pieces(targets_ref[...], 3)]
    have = sum(r.shape[0] for r in base)
    whole = have // 8 * 8
    both = jnp.concatenate(base, axis=0)
    top, rest = both[:whole], both[whole:]
    flat = up(branches * cut, q)
    for j in range(peers):
        line = [s[k : k + 1, j * cut : (j + 1) * cut] for k in range(branches)]
        if flat > branches * cut:
            line.append(jnp.zeros((1, flat - branches * cut), F32))
        line = jnp.concatenate(line, axis=1)
        tail = [rest] + [line[:, c : c + q] for c in range(0, flat, q)]
        out_ref[j] = jnp.concatenate([top, stack(tail, rows - whole)], axis=0).astype(BF)


def latent_kernel(
    row, cut_row, ahead,
    got_ref, turned_ref, w_hbm, bias_hbm, w2_hbm, b2_hbm, w1_hbm, b1_hbm,
    early_ref, mixed_ref, offset_ref, *refs,
):
    h_ref = refs[0] if ahead else None
    w_ref, bias_ref, w2_ref, b2_ref, w1_ref, b1_ref, sems = refs[-7:]
    chunks, _, q = got_ref.shape
    funcs = turned_ref.shape[1]
    branches, sensor_count, width = w_ref.shape
    dims = w1_ref.shape[0]
    per = sensor_count // q
    small = fetch(sems, 0, (w1_hbm, w1_ref), (b1_hbm, b1_ref), (bias_hbm, bias_ref), (b2_hbm, b2_ref))
    parts = [(k, pl.ds(c * q, q)) for k in range(branches) for c in range(per)]
    large = fetch(sems, 4, *[(w_hbm.at[p], w_ref.at[p]) for p in parts], (w2_hbm, w2_ref))
    wait(small)

    if ahead:
        first = first_layer(w1_ref, b1_ref)
        for j in range(chunks):
            h_ref[j] = hidden_units(got_ref[j].astype(F32)[row : row + dims], first)

    lats = []
    for k in range(branches):
        pre = bias_ref[k : k + 1, :]
        for c in range(per):
            large[k * per + c].wait()
            pre = pre + dot(turned_ref[k * per + c], w_ref[k, c * q : (c + 1) * q])
        lats.append(jnp.tanh(pre).astype(BF).astype(F32))
    product = (lats[0] * lats[1] * lats[2]).astype(BF)
    lines = [turned_ref[cut_row + c].astype(F32) for c in range(up(branches * sensor_count // funcs, q) // q)]
    if len(lines) * q < width:
        lines.append(jnp.zeros((funcs, width - len(lines) * q), F32))
    early_ref[...] = jnp.concatenate(lats + [jnp.concatenate(lines, axis=1)], axis=0).astype(BF)
    offset = jnp.sum(product.astype(F32) * b2_ref[...], axis=1, keepdims=True)
    offset_ref[...] = jnp.broadcast_to(offset, offset_ref.shape)
    large[-1].wait()
    mixed_ref[...] = dot(product, w2_ref[...], ((1,), (1,)))


def trunk_kernel(
    row, dims, total_funcs, ahead,
    got_ref, mixed_ref, offset_ref, *refs,
):
    if ahead:
        h_ref, late_ref, g_ref, m_ref, r_ref = refs
        unroll = h_ref.shape[0]
    else:
        w1_ref, b1_ref, late_ref, g_ref, m_ref, r_ref, h_ref = refs
        first = first_layer(w1_ref, b1_ref)
        unroll = h_ref.shape[0]
    chunks, _, q = got_ref.shape
    funcs, width = mixed_ref.shape
    scale = width ** (-0.5)
    mixed = jnp.concatenate(pieces(mixed_ref[...], 2), axis=0)
    offset = offset_ref[:, 0:1]
    place = lax.broadcasted_iota(jnp.int32, (funcs, q), 0).astype(F32)
    g_ref[...] = jnp.zeros_like(g_ref)
    m_ref[...] = jnp.zeros_like(m_ref)
    r_ref[...] = jnp.zeros_like(r_ref)

    def visit(j, slot):
        block = got_ref[j].astype(F32)
        xyz = block[row : row + dims]
        owner = block[row + dims : row + dims + 1]
        target = block[row + dims + 1 : row + dims + 2]
        target = target + block[row + dims + 2 : row + dims + 3]
        target = target + block[row + dims + 3 : row + dims + 4]
        if not ahead:
            h_ref[slot] = hidden_units(xyz, first)
        h = h_ref[slot]
        scores = dot(mixed, h, ((1,), (1,)))
        scores = scores[:funcs] + scores[funcs:] + offset
        owned = (owner == place).astype(F32)
        pred = jnp.sum(owned * scores, axis=0, keepdims=True) * scale
        resid = (pred - target) / total_funcs
        coef = owned * (resid * scale)
        g_ref[...] += dot(jnp.concatenate(pieces(coef, 2), axis=0), h)
        hf = h.astype(F32)
        slope = (1.0 - hf * hf).astype(BF)
        spread = jnp.concatenate([coef] + [coef * xyz[d : d + 1] for d in range(dims)], axis=0)
        m_ref[...] += dot(jnp.concatenate(pieces(spread, 2), axis=0), slope)
        r_ref[...] += coef

    for_chunks(chunks, unroll, visit)

    g = g_ref[:funcs] + g_ref[funcs:]
    r = jnp.broadcast_to(jnp.sum(r_ref[...], axis=1, keepdims=True), (funcs, late_ref.shape[1] - width))
    high, low = pieces(r, 2)
    lane = lax.broadcasted_iota(jnp.int32, r.shape, 1)
    r = jnp.where(lane < r.shape[1] // 2, high.astype(F32), low.astype(F32))
    half = (dims + 1) * funcs
    moments = m_ref[:half] + m_ref[half:]
    grads = [
        jnp.sum(moments[d * funcs : (d + 1) * funcs] * mixed_ref[...], axis=0, keepdims=True)
        for d in range(dims + 1)
    ]
    grads = jnp.concatenate(grads, axis=0)
    grads = jnp.concatenate([grads, jnp.zeros((dims + 1, r.shape[1]), F32)], axis=1)
    late_ref[...] = stack([jnp.concatenate([g, r], axis=1), grads], late_ref.shape[0]).astype(BF)


def factor_kernel(groups, funcs, *refs):
    earlies = refs[:groups]
    w2_hbm, b2_hbm, product_ref, factor_ref, turned_ref, w2_ref, b2_ref, sems = refs[groups:]
    copies = fetch(sems, 0, (w2_hbm, w2_ref), (b2_hbm, b2_ref))
    branches, cut, _ = turned_ref.shape
    early = [e[...].astype(F32) for e in earlies]

    def rows(first):
        return jnp.concatenate([p[first : first + funcs] for p in early], axis=0)

    lat = [rows(k * funcs) for k in range(branches)]
    product_ref[...] = (lat[0] * lat[1] * lat[2]).astype(BF)
    lines = rows(branches * funcs)
    for k in range(branches):
        others = [lat[j] for j in range(branches) if j != k]
        factor_ref[k] = others[0] * others[1] * (1.0 - lat[k] * lat[k])
        turned_ref[k] = lines[:, k * cut : (k + 1) * cut].T.astype(BF)
    wait(copies)


def tail_kernel(groups, funcs, dims, *refs):
    lates = refs[:groups]
    (
        product_ref, factor_ref, turned_ref, w2_ref, b2_ref,
        gbw_ref, gbb_ref, gw1_ref, gb1_ref, gw2_ref, gb2_ref, gbw_buf, gw2_buf, sems,
    ) = refs[groups:]
    width = w2_ref.shape[1]
    branches = gbw_ref.shape[0]
    late = [x[...].astype(F32) for x in lates]
    product = product_ref[...]
    ends = jnp.concatenate([x[:funcs] for x in late], axis=0)
    g, r = ends[:, :width], ends[:, width:]
    r = r[:, :1] + r[:, r.shape[1] // 2 : r.shape[1] // 2 + 1]
    copies = []
    blocks, height, _ = gw2_buf.shape
    for c in range(blocks):
        gw2_buf[c] = dot(g[:, c * height : (c + 1) * height].T.astype(BF), product)
        copies += fetch(sems, c, (gw2_buf.at[c], gw2_ref.at[pl.ds(c * height, height)]))
    dprod = dot(g.astype(BF), w2_ref[...]) + r * b2_ref[...]
    gbb = []
    for k in range(branches):
        delta = (dprod * factor_ref[k]).astype(BF)
        gbw_buf[k] = dot(turned_ref[k], delta)
        copies += fetch(sems, blocks + k, (gbw_buf.at[k], gbw_ref.at[k]))
        gbb.append(jnp.sum(delta.astype(F32), axis=0, keepdims=True))
    gbb_ref[...] = jnp.concatenate(gbb, axis=0)
    grads = late[0][funcs : funcs + dims + 1, :width]
    for x in late[1:]:
        grads = grads + x[funcs : funcs + dims + 1, :width]
    gb1_ref[...] = grads[:1]
    gw1_ref[...] = grads[1:]
    gb2_ref[...] = jnp.sum(r * product.astype(F32), axis=0, keepdims=True)
    wait(copies)


def shards(
    sensors, branch_w, branch_b, coords, func_index, targets, trunk_w1, trunk_b1, trunk_w2, trunk_b2
):
    branches, func_dev, sensor_count = sensors.shape
    dims, queries = coords.shape
    hidden, width = trunk_w2.shape
    nb, nq = lax.axis_size("branch"), lax.axis_size("query")
    assert func_dev == 1 and sensor_count % queries == 0 and hidden == width
    funcs = nq
    cut = sensor_count // nq
    per = sensor_count // queries
    row = branches * per
    cut_row = row + dims + 4
    rows = up(cut_row + up(branches * cut, queries) // queries, 8)
    ahead = nq * queries * hidden * 2 <= 16 * MIB
    units_shape = (nq if ahead else min(nq, 8), queries, hidden)

    packed = pl.pallas_call(
        pack_kernel,
        out_shape=jax.ShapeDtypeStruct((nq, rows, queries), BF),
        in_specs=[HBM] * 4,
        out_specs=VMEM,
        scratch_shapes=[
            pltpu.VMEM((branches, sensor_count), BF),
            pltpu.VMEM((dims, queries), BF),
            pltpu.VMEM((1, queries), jnp.int32),
            pltpu.VMEM((1, queries), F32),
            pltpu.SemaphoreType.DMA((4,)),
        ],
        compiler_params=pltpu.CompilerParams(vmem_limit_bytes=8 * MIB),
        name="pack",
    )(*in_hbm(sensors.reshape(branches, sensor_count), coords, func_index[None], targets[None]))
    got = lax.all_to_all(packed, "query", 0, 0, tiled=True)

    early, mixed, offset, *units = pl.pallas_call(
        functools.partial(latent_kernel, row, cut_row, ahead),
        out_shape=(
            jax.ShapeDtypeStruct(((branches + 1) * funcs, width), BF),
            jax.ShapeDtypeStruct((funcs, hidden), F32),
            jax.ShapeDtypeStruct((funcs, 128), F32),
        ) + (jax.ShapeDtypeStruct(units_shape, BF),) * ahead,
        in_specs=[VMEM] * 2 + [HBM] * 6,
        out_specs=(VMEM,) * (3 + ahead),
        scratch_shapes=[
            pltpu.VMEM((branches, sensor_count, width), BF),
            pltpu.VMEM((branches, width), F32),
            pltpu.VMEM((hidden, width), BF),
            pltpu.VMEM((1, width), F32),
            pltpu.VMEM((dims, hidden), BF),
            pltpu.VMEM((1, hidden), F32),
            pltpu.SemaphoreType.DMA((4 + branches * per + 1,)),
        ],
        compiler_params=pltpu.CompilerParams(vmem_limit_bytes=28 * MIB),
        cost_estimate=pl.CostEstimate(
            flops=2 * (256 * nq * queries * hidden + 256 * branch_w.size),
            bytes_accessed=2 * branch_w.size,
            transcendentals=nq * queries * hidden,
        ),
        name="latents",
    )(
        got,
        got.transpose(1, 0, 2),
        *in_hbm(branch_w, branch_b, trunk_w2, trunk_b2[None], trunk_w1, trunk_b1[None]),
    )

    needs = units if ahead else [trunk_w1, trunk_b1[None]]
    late_rows = up(funcs + dims + 1, 16)
    late = pl.pallas_call(
        functools.partial(trunk_kernel, row, dims, nb * nq, ahead),
        out_shape=jax.ShapeDtypeStruct((late_rows, width + 128), BF),
        in_specs=[VMEM] * (3 + len(needs)),
        out_specs=VMEM,
        scratch_shapes=[
            pltpu.VMEM((2 * funcs, hidden), F32),
            pltpu.VMEM((2 * (dims + 1) * funcs, hidden), F32),
            pltpu.VMEM((funcs, queries), F32),
        ] + [pltpu.VMEM(units_shape, BF)] * (not ahead),
        compiler_params=pltpu.CompilerParams(vmem_limit_bytes=24 * MIB),
        cost_estimate=pl.CostEstimate(
            flops=2 * 768 * nq * queries * hidden, bytes_accessed=2 * MIB, transcendentals=0
        ),
        name="trunk",
    )(got, mixed, offset, *needs)

    def gather(x):
        shifts = [[(i, (i + k) % nb) for i in range(nb)] for k in range(1, nb)]
        return [x] + [lax.ppermute(x, "branch", pairs) for pairs in shifts]

    earlies, lates = gather(early), gather(late)
    every = nb * funcs
    prepared = pl.pallas_call(
        functools.partial(factor_kernel, nb, funcs),
        out_shape=(
            jax.ShapeDtypeStruct((every, width), BF),
            jax.ShapeDtypeStruct((branches, every, width), F32),
            jax.ShapeDtypeStruct((branches, cut, every), BF),
            jax.ShapeDtypeStruct((hidden, width), BF),
            jax.ShapeDtypeStruct((1, width), F32),
        ),
        in_specs=[VMEM] * nb + [HBM] * 2,
        out_specs=(VMEM,) * 5,
        scratch_shapes=[pltpu.SemaphoreType.DMA((2,))],
        compiler_params=pltpu.CompilerParams(vmem_limit_bytes=16 * MIB),
        cost_estimate=pl.CostEstimate(flops=MIB, bytes_accessed=4 * MIB, transcendentals=0),
        name="factors",
    )(*earlies, *in_hbm(trunk_w2, trunk_b2[None]))
    blocks = 4
    gbw, gbb, gw1, gb1, gw2, gb2 = pl.pallas_call(
        functools.partial(tail_kernel, nb, funcs, dims),
        out_shape=(
            jax.ShapeDtypeStruct((branches, cut, width), F32),
            jax.ShapeDtypeStruct((branches, width), F32),
            jax.ShapeDtypeStruct((dims, hidden), F32),
            jax.ShapeDtypeStruct((1, hidden), F32),
            jax.ShapeDtypeStruct((hidden, width), F32),
            jax.ShapeDtypeStruct((1, width), F32),
        ),
        in_specs=[VMEM] * (nb + 5),
        out_specs=(HBM, VMEM, VMEM, VMEM, HBM, VMEM),
        scratch_shapes=[
            pltpu.VMEM((branches, cut, width), F32),
            pltpu.VMEM((blocks, hidden // blocks, width), F32),
            pltpu.SemaphoreType.DMA((blocks + branches,)),
        ],
        compiler_params=pltpu.CompilerParams(vmem_limit_bytes=24 * MIB),
        name="tail",
    )(*lates, *prepared)
    return (gbw, gbb, gw1, gb1[0], gw2, gb2[0])


def solution(mesh):
    placed = (
        P(None, ("branch", "query"), None),
        P(),
        P(),
        P(None, ("branch", "query")),
        P(("branch", "query")),
        P(("branch", "query")),
        P(),
        P(),
        P(),
        P(),
    )
    return jax.shard_map(
        shards,
        mesh=mesh,
        in_specs=placed,
        out_specs=(P(None, "query", None), P(), P(), P(), P(), P()),
        check_vma=False,
    )
```

```python
import functools

import jax
import jax.numpy as jnp
from jax import lax
from jax.experimental import pallas as pl
from jax.experimental.pallas import tpu as pltpu
from jax.sharding import PartitionSpec as P

BF = jnp.bfloat16
F32 = jnp.float32
MIB = 1 << 20
VMEM = pl.BlockSpec(memory_space=pltpu.VMEM)
HBM = pl.BlockSpec(memory_space=pltpu.HBM)


def up(value, step):
    return -(-value // step) * step


def pieces(value, count):
    out = []
    for _ in range(count):
        top = value.astype(BF)
        out.append(top)
        value = value - top.astype(F32)
    return out


def dot(a, b, dims=((1,), (0,))):
    return lax.dot_general(a, b, (dims, ((), ())), preferred_element_type=F32)


def stack(rows, count):
    have = sum(r.shape[0] for r in rows)
    if have < count:
        rows = rows + [jnp.zeros((count - have, rows[0].shape[1]), rows[0].dtype)]
    return jnp.concatenate(rows, axis=0)


def in_hbm(*arrays):
    return [pltpu.with_memory_space_constraint(a, pltpu.HBM) for a in arrays]


def first_layer(w1_ref, b1_ref):
    rows = [w1_ref[...].astype(F32)] + [b.astype(F32) for b in pieces(b1_ref[...], 3)]
    return stack(rows, up(w1_ref.shape[0] + 3, 8)).astype(BF)


def hidden_units(xyz, first):
    a = stack([xyz, jnp.ones((3, xyz.shape[1]), F32)], first.shape[0]).T.astype(BF)
    return jnp.tanh(dot(a, first)).astype(BF)


def fetch(sems, first, *pairs):
    copies = [pltpu.make_async_copy(src, dst, sems.at[first + i]) for i, (src, dst) in enumerate(pairs)]
    for copy in copies:
        copy.start()
    return copies


def wait(copies):
    for copy in copies:
        copy.wait()


LANES = 128


def plan(branches, sensor_count, dims, q, peers):
    row = branches * sensor_count // q
    cut = branches * (sensor_count // peers)
    side = 2 * q // LANES + up(cut, LANES) // LANES
    return row, up(max(row + dims + 1, side), 8)


def pack_kernel(
    row, sensors_hbm, coords_hbm, index_hbm, targets_hbm, out_ref, sensors_ref, coords_ref, index_ref, targets_ref, sems
):
    wait(fetch(
        sems, 0, (sensors_hbm, sensors_ref), (coords_hbm, coords_ref), (index_hbm, index_ref), (targets_hbm, targets_ref)
    ))
    peers, rows, _ = out_ref.shape
    q = coords_ref.shape[1]
    branches, sensor_count = sensors_ref.shape
    cut = sensor_count // peers
    s = sensors_ref[...].astype(F32)
    base = [s[k : k + 1, c : c + q] for k in range(branches) for c in range(0, sensor_count, q)]
    base += [coords_ref[...].astype(F32), index_ref[...].astype(F32)]
    base = stack(base, rows)
    targets = jnp.concatenate([t.astype(F32) for t in pieces(targets_ref[...], 2)], axis=1)
    targets = [targets[:, c : c + LANES] for c in range(0, 2 * q, LANES)]
    flat = up(branches * cut, LANES)
    for j in range(peers):
        line = [s[k : k + 1, j * cut : (j + 1) * cut] for k in range(branches)]
        if flat > branches * cut:
            line.append(jnp.zeros((1, flat - branches * cut), F32))
        line = jnp.concatenate(line, axis=1)
        side = stack(targets + [line[:, c : c + LANES] for c in range(0, flat, LANES)], rows)
        out_ref[j] = jnp.concatenate([base, side], axis=1).astype(BF)


def load_kernel(*refs):
    count = len(refs) // 2
    wait(fetch(refs[-1], 0, *zip(refs[:count], refs[count:-1])))


def latent_kernel(
    row, ahead,
    got_ref, turned_ref, bias_ref, w2_ref, b2_ref, w1_ref, b1_ref, w_hbm,
    early_ref, mixed_ref, offset_ref, *refs,
):
    w_ref, sems = refs[-2:]
    chunks = got_ref.shape[0]
    q = got_ref.shape[2] - LANES
    funcs = turned_ref.shape[1]
    branches, sensor_count, width = w_ref.shape
    dims = w1_ref.shape[0]
    parts = [(k, c) for k in range(branches) for c in range(0, sensor_count, q)]
    copies = fetch(sems, 0, *[(w_hbm.at[k, pl.ds(c, q)], w_ref.at[k, pl.ds(c, q)]) for k, c in parts])
    pre = [bias_ref[k : k + 1, :] for k in range(branches)]

    def multiply(i):
        k, c = parts[i]
        copies[i].wait()
        pre[k] = pre[k] + dot(turned_ref[i, :, :q], w_ref[k, c : c + q])

    done = 0
    if ahead:
        first = first_layer(w1_ref, b1_ref)
        for j in range(chunks):
            refs[0][j] = hidden_units(got_ref[j].astype(F32)[row : row + dims, :q], first)
            while done < len(parts) * max(j - 1, 0) // chunks:
                multiply(done)
                done += 1
    for i in range(done, len(parts)):
        multiply(i)
    lats = [jnp.tanh(p).astype(BF).astype(F32) for p in pre]
    product = (lats[0] * lats[1] * lats[2]).astype(BF)
    start = 2 * q // LANES
    flat = up(branches * sensor_count // chunks, LANES)
    lines = [turned_ref[start + c].astype(F32)[:, q:] for c in range(flat // LANES)]
    if flat < width:
        lines.append(jnp.zeros((funcs, width - flat), F32))
    early_ref[...] = jnp.concatenate(lats + [jnp.concatenate(lines, axis=1)], axis=0).astype(BF)
    offset = jnp.sum(product.astype(F32) * b2_ref[...], axis=1, keepdims=True)
    offset_ref[...] = jnp.broadcast_to(offset, offset_ref.shape)
    mixed_ref[...] = dot(product, w2_ref[...], ((1,), (1,)))


def trunk_kernel(
    row, dims, total_funcs, ahead,
    got_ref, mixed_ref, offset_ref, *refs,
):
    if ahead:
        h_ref, late_ref, g_ref, m_ref, r_ref, coef_ref = refs
    else:
        w1_ref, b1_ref, late_ref, g_ref, m_ref, r_ref, coef_ref, h_ref = refs
        first = first_layer(w1_ref, b1_ref)
    chunks = got_ref.shape[0]
    q = got_ref.shape[2] - LANES
    at_once = h_ref.shape[0]
    funcs, width = mixed_ref.shape
    scale = width ** (-0.5)
    mixed = jnp.concatenate(pieces(mixed_ref[...], 2), axis=0)
    offset = offset_ref[:, 0:1]
    place = lax.broadcasted_iota(jnp.int32, (funcs, q), 0).astype(F32)
    one = jnp.ones((), BF)
    g_ref[...] = jnp.zeros_like(g_ref)
    m_ref[...] = jnp.zeros_like(m_ref)
    r_ref[...] = jnp.zeros_like(r_ref)

    def residuals(j, slot):
        block = got_ref[j].astype(F32)
        xyz = block[row : row + dims, :q]
        owner = block[row + dims : row + dims + 1, :q]
        target = jnp.concatenate([block[c : c + 1, q:] for c in range(2 * q // LANES)], axis=1)
        target = target[:, :q] + target[:, q:]
        if not ahead:
            h_ref[slot] = hidden_units(xyz, first)
        scores = dot(mixed, h_ref[slot], ((1,), (1,)))
        scores = scores[:funcs] + scores[funcs:] + offset
        owned = (owner == place).astype(F32)
        pred = jnp.sum(owned * scores, axis=0, keepdims=True) * scale
        resid = (pred - target) / total_funcs
        coef = owned * (resid * scale)
        spread = jnp.concatenate([coef] + [coef * xyz[d : d + 1] for d in range(dims)], axis=0)
        coef_ref[slot] = jnp.concatenate(pieces(coef, 2) + pieces(spread, 2), axis=0)
        return coef

    def batch(start):
        r = r_ref[...]
        for slot in range(at_once):
            r = r + residuals(start + slot, slot)
        r_ref[...] = r
        g, m = g_ref[...], m_ref[...]
        for slot in range(at_once):
            h = h_ref[slot]
            g = g + dot(coef_ref[slot, : 2 * funcs], h)
            m = m + dot(coef_ref[slot, 2 * funcs :], (one - h) * (one + h))
        g_ref[...] = g
        m_ref[...] = m

    if chunks == at_once:
        batch(0)
    else:
        lax.fori_loop(0, chunks // at_once, lambda i, carry: (batch(i * at_once), carry)[1], 0)

    r = jnp.broadcast_to(jnp.sum(r_ref[...], axis=1, keepdims=True), (funcs, LANES))
    high, low = pieces(r, 2)
    lane = lax.broadcasted_iota(jnp.int32, r.shape, 1)
    r = jnp.where(lane < LANES // 2, high.astype(F32), low.astype(F32))
    half = (dims + 1) * funcs
    moments = m_ref[:half] + m_ref[half:]
    extra = late_ref.shape[1] - width - LANES
    grads = []
    for d in range(dims + 1):
        grad = jnp.sum(moments[d * funcs : (d + 1) * funcs] * mixed_ref[...], axis=0, keepdims=True)
        grads += [grad[:, c : c + extra] for c in range(0, grad.shape[1], extra)]
    late_ref[...] = jnp.concatenate([g_ref[:funcs] + g_ref[funcs:], r, stack(grads, funcs)], axis=1).astype(BF)


def factor_kernel(groups, funcs, *refs):
    earlies = refs[:groups]
    product_ref, factor_ref, turned_ref = refs[groups:]
    branches, cut, _ = turned_ref.shape
    early = [e[...].astype(F32) for e in earlies]

    def rows(first):
        return jnp.concatenate([p[first : first + funcs] for p in early], axis=0)

    lat = [rows(k * funcs) for k in range(branches)]
    product_ref[...] = (lat[0] * lat[1] * lat[2]).astype(BF)
    lines = rows(branches * funcs)
    for k in range(branches):
        others = [lat[j] for j in range(branches) if j != k]
        factor_ref[k] = others[0] * others[1] * (1.0 - lat[k] * lat[k])
        turned_ref[k] = lines[:, k * cut : (k + 1) * cut].T.astype(BF)


def tail_kernel(groups, funcs, dims, *refs):
    lates = refs[:groups]
    (
        product_ref, factor_ref, turned_ref, w2_ref, b2_ref,
        gbw_ref, gbb_ref, gw1_ref, gb1_ref, gw2_ref, gb2_ref, gbw_buf, gw2_buf, sems,
    ) = refs[groups:]
    width = w2_ref.shape[1]
    branches = gbw_ref.shape[0]
    late = [x[...].astype(F32) for x in lates]
    product = product_ref[...]
    g = jnp.concatenate([x[:, :width] for x in late], axis=0)
    r = jnp.concatenate([x[:, width : width + LANES] for x in late], axis=0)
    r = r[:, :1] + r[:, LANES // 2 : LANES // 2 + 1]
    copies = []
    blocks, height, _ = gw2_buf.shape
    for c in range(blocks):
        gw2_buf[c] = dot(g[:, c * height : (c + 1) * height].T.astype(BF), product)
        copies += fetch(sems, c, (gw2_buf.at[c], gw2_ref.at[pl.ds(c * height, height)]))
    dprod = dot(g.astype(BF), w2_ref[...]) + r * b2_ref[...]
    gbb = []
    for k in range(branches):
        delta = (dprod * factor_ref[k]).astype(BF)
        gbw_buf[k] = dot(turned_ref[k], delta)
        copies += fetch(sems, blocks + k, (gbw_buf.at[k], gbw_ref.at[k]))
        gbb.append(jnp.sum(delta.astype(F32), axis=0, keepdims=True))
    gbb_ref[...] = jnp.concatenate(gbb, axis=0)
    parts = late[0][:, width + LANES :]
    for x in late[1:]:
        parts = parts + x[:, width + LANES :]
    each = gw1_ref.shape[1] // parts.shape[1]
    grads = [
        jnp.concatenate([parts[d * each + c : d * each + c + 1] for c in range(each)], axis=1) for d in range(dims + 1)
    ]
    grads = jnp.concatenate(grads, axis=0)
    gb1_ref[...] = grads[:1]
    gw1_ref[...] = grads[1:]
    gb2_ref[...] = jnp.sum(r * product.astype(F32), axis=0, keepdims=True)
    wait(copies)


def shards(
    sensors, branch_w, branch_b, coords, func_index, targets, trunk_w1, trunk_b1, trunk_w2, trunk_b2
):
    branches, func_dev, sensor_count = sensors.shape
    dims, queries = coords.shape
    hidden, width = trunk_w2.shape
    nb, nq = lax.axis_size("branch"), lax.axis_size("query")
    assert func_dev == 1 and sensor_count % queries == 0 and hidden == width
    funcs = nq
    cut = sensor_count // nq
    row, rows = plan(branches, sensor_count, dims, queries, nq)
    ahead = nq * queries * hidden * 2 <= 16 * MIB
    units_shape = (nq if ahead else min(nq, 8), queries, hidden)

    packed = pl.pallas_call(
        functools.partial(pack_kernel, row),
        out_shape=jax.ShapeDtypeStruct((nq, rows, queries + LANES), BF),
        in_specs=[HBM] * 4,
        out_specs=VMEM,
        scratch_shapes=[
            pltpu.VMEM((branches, sensor_count), BF),
            pltpu.VMEM((dims, queries), BF),
            pltpu.VMEM((1, queries), jnp.int32),
            pltpu.VMEM((1, queries), F32),
            pltpu.SemaphoreType.DMA((4,)),
        ],
        compiler_params=pltpu.CompilerParams(vmem_limit_bytes=8 * MIB),
        name="pack",
    )(*in_hbm(sensors.reshape(branches, sensor_count), coords, func_index[None], targets[None]))
    got = lax.all_to_all(packed, "query", 0, 0, tiled=True)

    small = (branch_b, trunk_w2, trunk_b2[None], trunk_w1, trunk_b1[None])
    small = pl.pallas_call(
        load_kernel,
        out_shape=tuple(jax.ShapeDtypeStruct(x.shape, x.dtype) for x in small),
        in_specs=[HBM] * len(small),
        out_specs=(VMEM,) * len(small),
        scratch_shapes=[pltpu.SemaphoreType.DMA((len(small),))],
        compiler_params=pltpu.CompilerParams(vmem_limit_bytes=8 * MIB),
        cost_estimate=pl.CostEstimate(flops=0, bytes_accessed=4 * trunk_w2.size, transcendentals=0),
        name="load",
    )(*in_hbm(*small))
    early, mixed, offset, *units = pl.pallas_call(
        functools.partial(latent_kernel, row, ahead),
        out_shape=(
            jax.ShapeDtypeStruct(((branches + 1) * funcs, width), BF),
            jax.ShapeDtypeStruct((funcs, hidden), F32),
            jax.ShapeDtypeStruct((funcs, LANES), F32),
        ) + (jax.ShapeDtypeStruct(units_shape, BF),) * ahead,
        in_specs=[VMEM] * 7 + [HBM],
        out_specs=(VMEM,) * (3 + ahead),
        scratch_shapes=[
            pltpu.VMEM(branch_w.shape, BF),
            pltpu.SemaphoreType.DMA((row,)),
        ],
        compiler_params=pltpu.CompilerParams(vmem_limit_bytes=24 * MIB),
        cost_estimate=pl.CostEstimate(
            flops=2 * 256 * (nq * queries * hidden + branch_w.size), bytes_accessed=2 * branch_w.size, transcendentals=0
        ),
        name="latents",
    )(got, got.transpose(1, 0, 2), *small, *in_hbm(branch_w))

    needs = units if ahead else [trunk_w1, trunk_b1[None]]
    late_width = width + LANES + up(-(-(dims + 1) * hidden // funcs), LANES)
    late = pl.pallas_call(
        functools.partial(trunk_kernel, row, dims, nb * nq, ahead),
        out_shape=jax.ShapeDtypeStruct((funcs, late_width), BF),
        in_specs=[VMEM] * (3 + len(needs)),
        out_specs=VMEM,
        scratch_shapes=[
            pltpu.VMEM((2 * funcs, hidden), F32),
            pltpu.VMEM((2 * (dims + 1) * funcs, hidden), F32),
            pltpu.VMEM((funcs, queries), F32),
            pltpu.VMEM((units_shape[0], 2 * (dims + 2) * funcs, queries), BF),
        ] + [pltpu.VMEM(units_shape, BF)] * (not ahead),
        compiler_params=pltpu.CompilerParams(vmem_limit_bytes=24 * MIB),
        cost_estimate=pl.CostEstimate(
            flops=2 * 768 * nq * queries * hidden, bytes_accessed=2 * MIB, transcendentals=0
        ),
        name="trunk",
    )(got, mixed, offset, *needs)

    def gather(x):
        shifts = [[(i, (i + k) % nb) for i in range(nb)] for k in range(1, nb)]
        return [x] + [lax.ppermute(x, "branch", pairs) for pairs in shifts]

    earlies, lates = gather(early), gather(late)
    every = nb * funcs
    prepared = pl.pallas_call(
        functools.partial(factor_kernel, nb, funcs),
        out_shape=(
            jax.ShapeDtypeStruct((every, width), BF),
            jax.ShapeDtypeStruct((branches, every, width), F32),
            jax.ShapeDtypeStruct((branches, cut, every), BF),
        ),
        in_specs=[VMEM] * nb,
        out_specs=(VMEM,) * 3,
        compiler_params=pltpu.CompilerParams(vmem_limit_bytes=16 * MIB),
        cost_estimate=pl.CostEstimate(flops=MIB, bytes_accessed=4 * MIB, transcendentals=0),
        name="factors",
    )(*earlies)
    blocks = 4
    gbw, gbb, gw1, gb1, gw2, gb2 = pl.pallas_call(
        functools.partial(tail_kernel, nb, funcs, dims),
        out_shape=(
            jax.ShapeDtypeStruct((branches, cut, width), F32),
            jax.ShapeDtypeStruct((branches, width), F32),
            jax.ShapeDtypeStruct((dims, hidden), F32),
            jax.ShapeDtypeStruct((1, hidden), F32),
            jax.ShapeDtypeStruct((hidden, width), F32),
            jax.ShapeDtypeStruct((1, width), F32),
        ),
        in_specs=[VMEM] * (nb + 5),
        out_specs=(HBM, VMEM, VMEM, VMEM, HBM, VMEM),
        scratch_shapes=[
            pltpu.VMEM((branches, cut, width), F32),
            pltpu.VMEM((blocks, hidden // blocks, width), F32),
            pltpu.SemaphoreType.DMA((blocks + branches,)),
        ],
        compiler_params=pltpu.CompilerParams(vmem_limit_bytes=24 * MIB),
        name="tail",
    )(*lates, *prepared, small[1], small[2])
    return (gbw, gbb, gw1, gb1[0], gw2, gb2[0])


def solution(mesh):
    placed = (
        P(None, ("branch", "query"), None),
        P(),
        P(),
        P(None, ("branch", "query")),
        P(("branch", "query")),
        P(("branch", "query")),
        P(),
        P(),
        P(),
        P(),
    )
    return jax.shard_map(
        shards,
        mesh=mesh,
        in_specs=placed,
        out_specs=(P(None, "query", None), P(), P(), P(), P(), P()),
        check_vma=False,
    )
```

```python
import functools

import jax
import jax.numpy as jnp
from jax import lax
from jax.experimental import pallas as pl
from jax.experimental.pallas import tpu as pltpu
from jax.sharding import PartitionSpec as P

BF = jnp.bfloat16
F32 = jnp.float32
MIB = 1 << 20
VMEM = pl.BlockSpec(memory_space=pltpu.VMEM)
HBM = pl.BlockSpec(memory_space=pltpu.HBM)


def up(value, step):
    return -(-value // step) * step


def pieces(value, count):
    out = []
    for _ in range(count):
        top = value.astype(BF)
        out.append(top)
        value = value - top.astype(F32)
    return out


def dot(a, b, dims=((1,), (0,))):
    return lax.dot_general(a, b, (dims, ((), ())), preferred_element_type=F32)


def stack(rows, count):
    have = sum(r.shape[0] for r in rows)
    if have < count:
        rows = rows + [jnp.zeros((count - have, rows[0].shape[1]), rows[0].dtype)]
    return jnp.concatenate(rows, axis=0)


def in_hbm(*arrays):
    return [pltpu.with_memory_space_constraint(a, pltpu.HBM) for a in arrays]


def first_layer(w1_ref, b1_ref):
    rows = [w1_ref[...].astype(F32)] + [b.astype(F32) for b in pieces(b1_ref[...], 3)]
    return stack(rows, up(w1_ref.shape[0] + 3, 8)).astype(BF)


def hidden_units(xyz, first):
    a = stack([xyz, jnp.ones((3, xyz.shape[1]), F32)], first.shape[0]).T.astype(BF)
    return jnp.tanh(dot(a, first)).astype(BF)


def fetch(sems, first, *pairs):
    copies = [pltpu.make_async_copy(src, dst, sems.at[first + i]) for i, (src, dst) in enumerate(pairs)]
    for copy in copies:
        copy.start()
    return copies


def wait(copies):
    for copy in copies:
        copy.wait()


LANES = 128
BLOCKS = 8


def plan(branches, sensor_count, dims, q, peers):
    row = branches * sensor_count // q
    cut = branches * (sensor_count // peers)
    side = 2 * q // LANES + up(cut, LANES) // LANES
    return row, up(max(row + dims + 1, side), 8)


def pack_kernel(
    row, sensors_hbm, coords_hbm, index_hbm, targets_hbm, out_ref, sensors_ref, coords_ref, index_ref, targets_ref, sems
):
    wait(fetch(
        sems, 0, (sensors_hbm, sensors_ref), (coords_hbm, coords_ref), (index_hbm, index_ref), (targets_hbm, targets_ref)
    ))
    peers, rows, _ = out_ref.shape
    q = coords_ref.shape[1]
    branches, sensor_count = sensors_ref.shape
    cut = sensor_count // peers
    s = sensors_ref[...].astype(F32)
    base = [s[k : k + 1, c : c + q] for k in range(branches) for c in range(0, sensor_count, q)]
    base += [coords_ref[...].astype(F32), index_ref[...].astype(F32)]
    base = stack(base, rows)
    targets = jnp.concatenate([t.astype(F32) for t in pieces(targets_ref[...], 2)], axis=1)
    targets = [targets[:, c : c + LANES] for c in range(0, 2 * q, LANES)]
    flat = up(branches * cut, LANES)
    for j in range(peers):
        line = [s[k : k + 1, j * cut : (j + 1) * cut] for k in range(branches)]
        if flat > branches * cut:
            line.append(jnp.zeros((1, flat - branches * cut), F32))
        line = jnp.concatenate(line, axis=1)
        side = stack(targets + [line[:, c : c + LANES] for c in range(0, flat, LANES)], rows)
        out_ref[j] = jnp.concatenate([base, side], axis=1).astype(BF)


def load_kernel(*refs):
    count = len(refs) // 2
    pairs = list(zip(refs[: count - 1], refs[count:-2]))
    w_hbm, begun_ref = refs[count - 1], refs[-2]
    blocks, q, _ = begun_ref.shape
    each = w_hbm.shape[1] // q
    pairs += [(w_hbm.at[i // each, pl.ds(i % each * q, q)], begun_ref.at[i]) for i in range(blocks)]
    wait(fetch(refs[-1], 0, *pairs))


def latent_kernel(
    row, ahead,
    got_ref, turned_ref, bias_ref, b2_ref, w1_ref, b1_ref, begun_ref, w_hbm, w2_hbm,
    early_ref, mixed_ref, offset_ref, w2_ref, *refs,
):
    w_ref, sems = refs[-2:]
    chunks = got_ref.shape[0]
    q = got_ref.shape[2] - LANES
    funcs = turned_ref.shape[1]
    branches, sensor_count, width = w_ref.shape
    dims = w1_ref.shape[0]
    parts = [(k, c) for k in range(branches) for c in range(0, sensor_count, q)]
    begun = begun_ref.shape[0]
    copies = fetch(
        sems, 0, *[(w_hbm.at[k, pl.ds(c, q)], w_ref.at[k, pl.ds(c, q)]) for k, c in parts[begun:]], (w2_hbm, w2_ref)
    )
    pre = [bias_ref[k : k + 1, :] for k in range(branches)]

    def multiply(i):
        k, c = parts[i]
        if i < begun:
            block = begun_ref[i]
        else:
            copies[i - begun].wait()
            block = w_ref[k, c : c + q]
        pre[k] = pre[k] + dot(turned_ref[i, :, :q], block)

    done = 0
    if ahead:
        first = first_layer(w1_ref, b1_ref)
        for j in range(chunks):
            refs[0][j] = hidden_units(got_ref[j].astype(F32)[row : row + dims, :q], first)
            ready = begun + (len(parts) - begun) * max(j - 2, 0) // chunks
            while done < ready:
                multiply(done)
                done += 1
    for i in range(done, len(parts)):
        multiply(i)
    lats = [jnp.tanh(p).astype(BF).astype(F32) for p in pre]
    product = (lats[0] * lats[1] * lats[2]).astype(BF)
    start = 2 * q // LANES
    flat = early_ref.shape[1] - branches * width
    lines = [turned_ref[start + c].astype(F32)[:, q:] for c in range(flat // LANES)]
    early_ref[...] = jnp.concatenate(lats + lines, axis=1).astype(BF)
    offset = jnp.sum(product.astype(F32) * b2_ref[...], axis=1, keepdims=True)
    offset_ref[...] = jnp.broadcast_to(offset, offset_ref.shape)
    copies[-1].wait()
    mixed_ref[...] = dot(product, w2_ref[...], ((1,), (1,)))


def trunk_kernel(
    row, dims, total_funcs, ahead,
    got_ref, mixed_ref, offset_ref, early_ref, *refs,
):
    if ahead:
        h_ref, late_ref, g_ref, m_ref, r_ref, coef_ref = refs
    else:
        w1_ref, b1_ref, late_ref, g_ref, m_ref, r_ref, coef_ref, h_ref = refs
        first = first_layer(w1_ref, b1_ref)
    chunks = got_ref.shape[0]
    q = got_ref.shape[2] - LANES
    at_once = h_ref.shape[0]
    funcs, width = mixed_ref.shape
    scale = width ** (-0.5)
    mixed = jnp.concatenate(pieces(mixed_ref[...], 2), axis=0)
    offset = offset_ref[:, 0:1]
    place = lax.broadcasted_iota(jnp.int32, (funcs, q), 0).astype(F32)
    one = jnp.ones((), BF)
    g_ref[...] = jnp.zeros_like(g_ref)
    m_ref[...] = jnp.zeros_like(m_ref)
    r_ref[...] = jnp.zeros_like(r_ref)

    def residuals(j, slot):
        block = got_ref[j].astype(F32)
        xyz = block[row : row + dims, :q]
        owner = block[row + dims : row + dims + 1, :q]
        target = jnp.concatenate([block[c : c + 1, q:] for c in range(2 * q // LANES)], axis=1)
        target = target[:, :q] + target[:, q:]
        if not ahead:
            h_ref[slot] = hidden_units(xyz, first)
        scores = dot(mixed, h_ref[slot], ((1,), (1,)))
        scores = scores[:funcs] + scores[funcs:] + offset
        owned = (owner == place).astype(F32)
        pred = jnp.sum(owned * scores, axis=0, keepdims=True) * scale
        resid = (pred - target) / total_funcs
        coef = owned * (resid * scale)
        spread = jnp.concatenate([coef] + [coef * xyz[d : d + 1] for d in range(dims)], axis=0)
        coef_ref[slot] = jnp.concatenate(pieces(coef, 2) + pieces(spread, 2), axis=0)
        return coef

    def batch(start):
        r = r_ref[...]
        for slot in range(at_once):
            r = r + residuals(start + slot, slot)
        r_ref[...] = r
        g, m = g_ref[...], m_ref[...]
        for slot in range(at_once):
            h = h_ref[slot]
            g = g + dot(coef_ref[slot, : 2 * funcs], h)
            m = m + dot(coef_ref[slot, 2 * funcs :], (one - h) * (one + h))
        g_ref[...] = g
        m_ref[...] = m

    if chunks == at_once:
        batch(0)
    else:
        lax.fori_loop(0, chunks // at_once, lambda i, carry: (batch(i * at_once), carry)[1], 0)

    r = jnp.broadcast_to(jnp.sum(r_ref[...], axis=1, keepdims=True), (funcs, LANES))
    high, low = pieces(r, 2)
    lane = lax.broadcasted_iota(jnp.int32, r.shape, 1)
    r = jnp.where(lane < LANES // 2, high.astype(F32), low.astype(F32))
    half = (dims + 1) * funcs
    moments = m_ref[:half] + m_ref[half:]
    extra = late_ref.shape[1] - early_ref.shape[1] - width - LANES
    grads = []
    for d in range(dims + 1):
        grad = jnp.sum(moments[d * funcs : (d + 1) * funcs] * mixed_ref[...], axis=0, keepdims=True)
        grads += [grad[:, c : c + extra] for c in range(0, grad.shape[1], extra)]
    sums = jnp.concatenate([g_ref[:funcs] + g_ref[funcs:], r, stack(grads, funcs)], axis=1)
    late_ref[:, : sums.shape[1]] = sums.astype(BF)
    late_ref[:, sums.shape[1] :] = early_ref[...]


def tail_kernel(groups, early_width, *refs):
    w2_ref, b2_ref = refs[groups : groups + 2]
    outs, bufs, sems = refs[groups + 2 : groups + 8], refs[groups + 8 : groups + 14], refs[-1]
    gbw_ref, gbb_ref, gw1_ref, gb1_ref, gw2_ref, gb2_ref = bufs
    width = w2_ref.shape[1]
    branches, cut, _ = gbw_ref.shape
    dims = gw1_ref.shape[0]
    all_rows = [x[...].astype(F32) for x in refs[:groups]]
    ends = all_rows[0].shape[1] - early_width
    copies = []

    def send(index, *at):
        source, target = bufs[index], outs[index]
        if at:
            source, target = source.at[at], target.at[at]
        copies.extend(fetch(sems, len(copies), (source, target)))

    def columns(first, count):
        return jnp.concatenate([x[:, first : first + count] for x in all_rows], axis=0)

    lat = [columns(ends + k * width, width) for k in range(branches)]
    product = (lat[0] * lat[1] * lat[2]).astype(BF)
    g = columns(0, width).astype(BF)
    height = gw2_ref.shape[0] // BLOCKS
    for c in range(0, gw2_ref.shape[0], height):
        gw2_ref[c : c + height] = dot(g[:, c : c + height], product, ((0,), (0,)))
        send(4, pl.ds(c, height))
    r = columns(width, LANES)
    r = r[:, :1] + r[:, LANES // 2 : LANES // 2 + 1]
    dprod = dot(g, w2_ref[...]) + r * b2_ref[...]
    lines = columns(ends + branches * width, branches * cut)
    gbb = []
    for k in range(branches):
        others = [lat[j] for j in range(branches) if j != k]
        delta = (dprod * (others[0] * others[1] * (1.0 - lat[k] * lat[k]))).astype(BF)
        gbw_ref[k] = dot(lines[:, k * cut : (k + 1) * cut].astype(BF), delta, ((0,), (0,)))
        send(0, k)
        gbb.append(jnp.sum(delta.astype(F32), axis=0, keepdims=True))
    gbb_ref[...] = jnp.concatenate(gbb, axis=0)
    parts = all_rows[0][:, width + LANES : ends]
    for x in all_rows[1:]:
        parts = parts + x[:, width + LANES : ends]
    each = gw1_ref.shape[1] // parts.shape[1]
    grads = [
        jnp.concatenate([parts[d * each + c : d * each + c + 1] for c in range(each)], axis=1) for d in range(dims + 1)
    ]
    gb1_ref[...] = grads[0]
    gw1_ref[...] = jnp.concatenate(grads[1:], axis=0)
    gb2_ref[...] = jnp.sum(r * product.astype(F32), axis=0, keepdims=True)
    for index in (1, 2, 3, 5):
        send(index)
    wait(copies)


def shards(
    sensors, branch_w, branch_b, coords, func_index, targets, trunk_w1, trunk_b1, trunk_w2, trunk_b2
):
    branches, func_dev, sensor_count = sensors.shape
    dims, queries = coords.shape
    hidden, width = trunk_w2.shape
    nb, nq = lax.axis_size("branch"), lax.axis_size("query")
    assert func_dev == 1 and sensor_count % queries == 0 and hidden == width
    funcs = nq
    cut = sensor_count // nq
    row, rows = plan(branches, sensor_count, dims, queries, nq)
    ahead = nq * queries * hidden * 2 <= 16 * MIB
    units_shape = (nq if ahead else min(nq, 8), queries, hidden)

    packed = pl.pallas_call(
        functools.partial(pack_kernel, row),
        out_shape=jax.ShapeDtypeStruct((nq, rows, queries + LANES), BF),
        in_specs=[HBM] * 4,
        out_specs=VMEM,
        scratch_shapes=[
            pltpu.VMEM((branches, sensor_count), BF),
            pltpu.VMEM((dims, queries), BF),
            pltpu.VMEM((1, queries), jnp.int32),
            pltpu.VMEM((1, queries), F32),
            pltpu.SemaphoreType.DMA((4,)),
        ],
        compiler_params=pltpu.CompilerParams(vmem_limit_bytes=8 * MIB),
        name="pack",
    )(*in_hbm(sensors.reshape(branches, sensor_count), coords, func_index[None], targets[None]))
    got = lax.all_to_all(packed, "query", 0, 0, tiled=True)

    early_width = branches * width + up(branches * cut, LANES)
    sums_width = width + LANES + up(-(-(dims + 1) * hidden // funcs), LANES)
    begun = min(row, 3 * MIB // (2 * queries * width))

    small = (branch_b, trunk_b2[None], trunk_w1, trunk_b1[None])
    shapes = [jax.ShapeDtypeStruct(x.shape, x.dtype) for x in small]
    small = pl.pallas_call(
        load_kernel,
        out_shape=(*shapes, jax.ShapeDtypeStruct((begun, queries, width), BF)),
        in_specs=[HBM] * (len(small) + 1),
        out_specs=(VMEM,) * (len(small) + 1),
        scratch_shapes=[pltpu.SemaphoreType.DMA((len(small) + begun,))],
        compiler_params=pltpu.CompilerParams(vmem_limit_bytes=8 * MIB),
        cost_estimate=pl.CostEstimate(flops=0, bytes_accessed=4 * trunk_w2.size, transcendentals=0),
        name="load",
    )(*in_hbm(*small, branch_w))
    early, mixed, offset, w2_here, *units = pl.pallas_call(
        functools.partial(latent_kernel, row, ahead),
        out_shape=(
            jax.ShapeDtypeStruct((funcs, early_width), BF),
            jax.ShapeDtypeStruct((funcs, hidden), F32),
            jax.ShapeDtypeStruct((funcs, LANES), F32),
            jax.ShapeDtypeStruct((hidden, width), BF),
        ) + (jax.ShapeDtypeStruct(units_shape, BF),) * ahead,
        in_specs=[VMEM] * 7 + [HBM] * 2,
        out_specs=(VMEM,) * (4 + ahead),
        scratch_shapes=[
            pltpu.VMEM(branch_w.shape, BF),
            pltpu.SemaphoreType.DMA((row - begun + 1,)),
        ],
        compiler_params=pltpu.CompilerParams(vmem_limit_bytes=24 * MIB),
        cost_estimate=pl.CostEstimate(
            flops=2 * 256 * (nq * queries * hidden + branch_w.size), bytes_accessed=2 * branch_w.size, transcendentals=0
        ),
        name="latents",
    )(got, got.transpose(1, 0, 2), *small, *in_hbm(branch_w, trunk_w2))

    needs = units if ahead else [trunk_w1, trunk_b1[None]]
    sums = pl.pallas_call(
        functools.partial(trunk_kernel, row, dims, nb * nq, ahead),
        out_shape=jax.ShapeDtypeStruct((funcs, sums_width + early_width), BF),
        in_specs=[VMEM] * (4 + len(needs)),
        out_specs=VMEM,
        scratch_shapes=[
            pltpu.VMEM((2 * funcs, hidden), F32),
            pltpu.VMEM((2 * (dims + 1) * funcs, hidden), F32),
            pltpu.VMEM((funcs, queries), F32),
            pltpu.VMEM((units_shape[0], 2 * (dims + 2) * funcs, queries), BF),
        ] + [pltpu.VMEM(units_shape, BF)] * (not ahead),
        compiler_params=pltpu.CompilerParams(vmem_limit_bytes=24 * MIB),
        cost_estimate=pl.CostEstimate(
            flops=2 * 768 * nq * queries * hidden, bytes_accessed=2 * MIB, transcendentals=0
        ),
        name="trunk",
    )(got, mixed, offset, early, *needs)

    def shift(x, k):
        return lax.ppermute(x, "branch", [(i, (i + k) % nb) for i in range(nb)])

    def swap(x):
        return lax.ppermute(x, "branch", [(i, i ^ 1) for i in range(nb)])

    if nb % 2:
        every = [sums] + [shift(sums, k) for k in range(1, nb)]
    else:
        every = [sums] + [shift(sums, k) for k in range(2, nb, 2)]
        every += [swap(x) for x in every]
    outs = (
        jax.ShapeDtypeStruct((branches, cut, width), F32),
        jax.ShapeDtypeStruct((branches, width), F32),
        jax.ShapeDtypeStruct((dims, hidden), F32),
        jax.ShapeDtypeStruct((1, hidden), F32),
        jax.ShapeDtypeStruct((hidden, width), F32),
        jax.ShapeDtypeStruct((1, width), F32),
    )
    gbw, gbb, gw1, gb1, gw2, gb2 = pl.pallas_call(
        functools.partial(tail_kernel, nb, early_width),
        out_shape=outs,
        in_specs=[VMEM] * (nb + 2),
        out_specs=(HBM,) * len(outs),
        scratch_shapes=[pltpu.VMEM(x.shape, F32) for x in outs]
        + [pltpu.SemaphoreType.DMA((BLOCKS + branches + 4,))],
        compiler_params=pltpu.CompilerParams(vmem_limit_bytes=24 * MIB),
        name="tail",
    )(*every, w2_here, small[1])
    return (gbw, gbb, gw1, gb1[0], gw2, gb2[0])


def solution(mesh):
    placed = (
        P(None, ("branch", "query"), None),
        P(),
        P(),
        P(None, ("branch", "query")),
        P(("branch", "query")),
        P(("branch", "query")),
        P(),
        P(),
        P(),
        P(),
    )
    return jax.shard_map(
        shards,
        mesh=mesh,
        in_specs=placed,
        out_specs=(P(None, "query", None), P(), P(), P(), P(), P()),
        check_vma=False,
    )
```

```python
import functools

import jax
import jax.numpy as jnp
from jax import lax
from jax.experimental import pallas as pl
from jax.experimental.pallas import tpu as pltpu
from jax.sharding import PartitionSpec as P

BF = jnp.bfloat16
F32 = jnp.float32
MIB = 1 << 20
VMEM = pl.BlockSpec(memory_space=pltpu.VMEM)
HBM = pl.BlockSpec(memory_space=pltpu.HBM)


def up(value, step):
    return -(-value // step) * step


def pieces(value, count):
    out = []
    for _ in range(count):
        top = value.astype(BF)
        out.append(top)
        value = value - top.astype(F32)
    return out


def dot(a, b, dims=((1,), (0,))):
    return lax.dot_general(a, b, (dims, ((), ())), preferred_element_type=F32)


def stack(rows, count):
    have = sum(r.shape[0] for r in rows)
    if have < count:
        rows = rows + [jnp.zeros((count - have, rows[0].shape[1]), rows[0].dtype)]
    return jnp.concatenate(rows, axis=0)


def in_hbm(*arrays):
    return [pltpu.with_memory_space_constraint(a, pltpu.HBM) for a in arrays]


def first_layer(w1_ref, b1_ref):
    rows = [w1_ref[...].astype(F32)] + [b.astype(F32) for b in pieces(b1_ref[...], 3)]
    return stack(rows, up(w1_ref.shape[0] + 3, 8)).astype(BF)


def hidden_units(xyz, first):
    a = stack([xyz, jnp.ones((3, xyz.shape[1]), F32)], first.shape[0]).T.astype(BF)
    return jnp.tanh(dot(a, first)).astype(BF)


def fetch(sems, first, *pairs):
    copies = [pltpu.make_async_copy(src, dst, sems.at[first + i]) for i, (src, dst) in enumerate(pairs)]
    for copy in copies:
        copy.start()
    return copies


def wait(copies):
    for copy in copies:
        copy.wait()


LANES = 128
BLOCKS = 8


def plan(branches, sensor_count, dims, q, peers):
    row = branches * sensor_count // q
    cut = branches * (sensor_count // peers)
    side = 2 * q // LANES + up(cut, LANES) // LANES
    return row, up(max(row + dims + 1, side), 8)


def pack_kernel(
    row, sensors_hbm, coords_hbm, index_hbm, targets_hbm, out_ref, sensors_ref, coords_ref, index_ref, targets_ref, sems
):
    wait(fetch(
        sems, 0, (sensors_hbm, sensors_ref), (coords_hbm, coords_ref), (index_hbm, index_ref), (targets_hbm, targets_ref)
    ))
    peers, rows, _ = out_ref.shape
    q = coords_ref.shape[1]
    branches, sensor_count = sensors_ref.shape
    cut = sensor_count // peers
    s = sensors_ref[...].astype(F32)
    base = [s[k : k + 1, c : c + q] for k in range(branches) for c in range(0, sensor_count, q)]
    base += [coords_ref[...].astype(F32), index_ref[...].astype(F32)]
    base = stack(base, rows)
    targets = jnp.concatenate([t.astype(F32) for t in pieces(targets_ref[...], 2)], axis=1)
    targets = [targets[:, c : c + LANES] for c in range(0, 2 * q, LANES)]
    flat = up(branches * cut, LANES)
    for j in range(peers):
        line = [s[k : k + 1, j * cut : (j + 1) * cut] for k in range(branches)]
        if flat > branches * cut:
            line.append(jnp.zeros((1, flat - branches * cut), F32))
        line = jnp.concatenate(line, axis=1)
        side = stack(targets + [line[:, c : c + LANES] for c in range(0, flat, LANES)], rows)
        out_ref[j] = jnp.concatenate([base, side], axis=1).astype(BF)


def load_kernel(*refs):
    count = len(refs) // 2
    pairs = list(zip(refs[: count - 1], refs[count:-2]))
    w_hbm, begun_ref = refs[count - 1], refs[-2]
    blocks, q, _ = begun_ref.shape
    each = w_hbm.shape[1] // q
    pairs += [(w_hbm.at[i // each, pl.ds(i % each * q, q)], begun_ref.at[i]) for i in range(blocks)]
    wait(fetch(refs[-1], 0, *pairs))


def group_kernel(
    row, total_funcs,
    got_ref, turned_ref, bias_ref, b2_ref, w1_ref, b1_ref, begun_ref, w_hbm, w2_hbm,
    out_ref, w2_ref,
    h_ref, w_ref, g_ref, m_ref, r_ref, coef_ref, sems,
):
    chunks = got_ref.shape[0]
    q = got_ref.shape[2] - LANES
    funcs = turned_ref.shape[1]
    branches, sensor_count, width = w_ref.shape
    dims, hidden = w1_ref.shape
    scale = width ** (-0.5)
    at_once = h_ref.shape[0]
    ahead = at_once == chunks
    parts = [(k, c) for k in range(branches) for c in range(0, sensor_count, q)]
    begun = begun_ref.shape[0]
    copies = fetch(
        sems, 0, *[(w_hbm.at[k, pl.ds(c, q)], w_ref.at[k, pl.ds(c, q)]) for k, c in parts[begun:]], (w2_hbm, w2_ref)
    )

    pre = [bias_ref[k : k + 1, :] for k in range(branches)]

    def multiply(i):
        k, c = parts[i]
        if i < begun:
            block = begun_ref[i]
        else:
            copies[i - begun].wait()
            block = w_ref[k, c : c + q]
        pre[k] = pre[k] + dot(turned_ref[i, :, :q], block)

    done = 0
    first = first_layer(w1_ref, b1_ref)
    if ahead:
        for j in range(chunks):
            h_ref[j] = hidden_units(got_ref[j].astype(F32)[row : row + dims, :q], first)
            ready = begun + (len(parts) - begun) * max(j - 2, 0) // chunks
            while done < ready:
                multiply(done)
                done += 1
    for i in range(done, len(parts)):
        multiply(i)
    lats = [jnp.tanh(p).astype(BF).astype(F32) for p in pre]
    product = (lats[0] * lats[1] * lats[2]).astype(BF)
    offset = jnp.sum(product.astype(F32) * b2_ref[...], axis=1, keepdims=True)
    copies[-1].wait()
    mixed_full = dot(product, w2_ref[...], ((1,), (1,)))
    mixed = jnp.concatenate(pieces(mixed_full, 2), axis=0)

    place = lax.broadcasted_iota(jnp.int32, (funcs, q), 0).astype(F32)
    one = jnp.ones((), BF)
    g_ref[...] = jnp.zeros_like(g_ref)
    m_ref[...] = jnp.zeros_like(m_ref)
    r_ref[...] = jnp.zeros_like(r_ref)

    def residuals(j, slot):
        block = got_ref[j].astype(F32)
        xyz = block[row : row + dims, :q]
        owner = block[row + dims : row + dims + 1, :q]
        target = jnp.concatenate([block[c : c + 1, q:] for c in range(2 * q // LANES)], axis=1)
        target = target[:, :q] + target[:, q:]
        if not ahead:
            h_ref[slot] = hidden_units(xyz, first)
        scores = dot(mixed, h_ref[slot], ((1,), (1,)))
        scores = scores[:funcs] + scores[funcs:] + offset
        owned = (owner == place).astype(F32)
        pred = jnp.sum(owned * scores, axis=0, keepdims=True) * scale
        resid = (pred - target) / total_funcs
        coef = owned * (resid * scale)
        spread = jnp.concatenate([coef] + [coef * xyz[d : d + 1] for d in range(dims)], axis=0)
        coef_ref[slot] = jnp.concatenate(pieces(coef, 2) + pieces(spread, 2), axis=0)
        return coef

    def batch(start):
        r = r_ref[...]
        for slot in range(at_once):
            r = r + residuals(start + slot, slot)
        r_ref[...] = r
        g, m = g_ref[...], m_ref[...]
        for slot in range(at_once):
            h = h_ref[slot]
            g = g + dot(coef_ref[slot, : 2 * funcs], h)
            m = m + dot(coef_ref[slot, 2 * funcs :], (one - h) * (one + h))
        g_ref[...] = g
        m_ref[...] = m

    if ahead:
        batch(0)
    else:
        lax.fori_loop(0, chunks // at_once, lambda i, carry: (batch(i * at_once), carry)[1], 0)

    r = jnp.broadcast_to(jnp.sum(r_ref[...], axis=1, keepdims=True), (funcs, LANES))
    high, low = pieces(r, 2)
    lane = lax.broadcasted_iota(jnp.int32, r.shape, 1)
    r = jnp.where(lane < LANES // 2, high.astype(F32), low.astype(F32))
    half = (dims + 1) * funcs
    moments = m_ref[:half] + m_ref[half:]
    extra = up(-(-(dims + 1) * hidden // funcs), LANES)
    grads = []
    for d in range(dims + 1):
        grad = jnp.sum(moments[d * funcs : (d + 1) * funcs] * mixed_full, axis=0, keepdims=True)
        grads += [grad[:, c : c + extra] for c in range(0, hidden, extra)]
    start = 2 * q // LANES
    flat = out_ref.shape[1] - width - LANES - extra - branches * width
    lines = [turned_ref[start + c].astype(F32)[:, q:] for c in range(flat // LANES)]
    sums = [g_ref[:funcs] + g_ref[funcs:], r, stack(grads, funcs)]
    out_ref[...] = jnp.concatenate(sums + lats + lines, axis=1).astype(BF)


def tail_kernel(groups, early_width, *refs):
    w2_ref, b2_ref = refs[groups : groups + 2]
    outs, bufs, sems = refs[groups + 2 : groups + 8], refs[groups + 8 : groups + 14], refs[-1]
    gbw_ref, gbb_ref, gw1_ref, gb1_ref, gw2_ref, gb2_ref = bufs
    width = w2_ref.shape[1]
    branches, cut, _ = gbw_ref.shape
    dims = gw1_ref.shape[0]
    all_rows = [x[...].astype(F32) for x in refs[:groups]]
    ends = all_rows[0].shape[1] - early_width
    copies = []

    def send(index, *at):
        source, target = bufs[index], outs[index]
        if at:
            source, target = source.at[at], target.at[at]
        copies.extend(fetch(sems, len(copies), (source, target)))

    def columns(first, count):
        return jnp.concatenate([x[:, first : first + count] for x in all_rows], axis=0)

    lat = [columns(ends + k * width, width) for k in range(branches)]
    product = (lat[0] * lat[1] * lat[2]).astype(BF)
    g = columns(0, width).astype(BF)
    height = gw2_ref.shape[0] // BLOCKS
    for c in range(0, gw2_ref.shape[0], height):
        gw2_ref[c : c + height] = dot(g[:, c : c + height], product, ((0,), (0,)))
        send(4, pl.ds(c, height))
    r = columns(width, LANES)
    r = r[:, :1] + r[:, LANES // 2 : LANES // 2 + 1]
    dprod = dot(g, w2_ref[...]) + r * b2_ref[...]
    lines = columns(ends + branches * width, branches * cut)
    gbb = []
    for k in range(branches):
        others = [lat[j] for j in range(branches) if j != k]
        delta = (dprod * (others[0] * others[1] * (1.0 - lat[k] * lat[k]))).astype(BF)
        gbw_ref[k] = dot(lines[:, k * cut : (k + 1) * cut].astype(BF), delta, ((0,), (0,)))
        send(0, k)
        gbb.append(jnp.sum(delta.astype(F32), axis=0, keepdims=True))
    gbb_ref[...] = jnp.concatenate(gbb, axis=0)
    parts = all_rows[0][:, width + LANES : ends]
    for x in all_rows[1:]:
        parts = parts + x[:, width + LANES : ends]
    each = gw1_ref.shape[1] // parts.shape[1]
    grads = [
        jnp.concatenate([parts[d * each + c : d * each + c + 1] for c in range(each)], axis=1) for d in range(dims + 1)
    ]
    gb1_ref[...] = grads[0]
    gw1_ref[...] = jnp.concatenate(grads[1:], axis=0)
    gb2_ref[...] = jnp.sum(r * product.astype(F32), axis=0, keepdims=True)
    for index in (1, 2, 3, 5):
        send(index)
    wait(copies)


def shards(
    sensors, branch_w, branch_b, coords, func_index, targets, trunk_w1, trunk_b1, trunk_w2, trunk_b2
):
    branches, func_dev, sensor_count = sensors.shape
    dims, queries = coords.shape
    hidden, width = trunk_w2.shape
    nb, nq = lax.axis_size("branch"), lax.axis_size("query")
    assert func_dev == 1 and sensor_count % queries == 0 and hidden == width
    funcs = nq
    cut = sensor_count // nq
    row, rows = plan(branches, sensor_count, dims, queries, nq)
    at_once = nq if nq * queries * hidden * 2 <= 16 * MIB else 8
    assert nq % at_once == 0

    packed = pl.pallas_call(
        functools.partial(pack_kernel, row),
        out_shape=jax.ShapeDtypeStruct((nq, rows, queries + LANES), BF),
        in_specs=[HBM] * 4,
        out_specs=VMEM,
        scratch_shapes=[
            pltpu.VMEM((branches, sensor_count), BF),
            pltpu.VMEM((dims, queries), BF),
            pltpu.VMEM((1, queries), jnp.int32),
            pltpu.VMEM((1, queries), F32),
            pltpu.SemaphoreType.DMA((4,)),
        ],
        compiler_params=pltpu.CompilerParams(vmem_limit_bytes=8 * MIB),
        name="pack",
    )(*in_hbm(sensors.reshape(branches, sensor_count), coords, func_index[None], targets[None]))
    got = lax.all_to_all(packed, "query", 0, 0, tiled=True)

    early_width = branches * width + up(branches * cut, LANES)
    sums_width = width + LANES + up(-(-(dims + 1) * hidden // funcs), LANES)
    begun = min(row, 3 * MIB // (2 * queries * width))

    small = (branch_b, trunk_b2[None], trunk_w1, trunk_b1[None])
    shapes = [jax.ShapeDtypeStruct(x.shape, x.dtype) for x in small]
    small = pl.pallas_call(
        load_kernel,
        out_shape=(*shapes, jax.ShapeDtypeStruct((begun, queries, width), BF)),
        in_specs=[HBM] * (len(small) + 1),
        out_specs=(VMEM,) * (len(small) + 1),
        scratch_shapes=[pltpu.SemaphoreType.DMA((len(small) + begun,))],
        compiler_params=pltpu.CompilerParams(vmem_limit_bytes=8 * MIB),
        cost_estimate=pl.CostEstimate(flops=0, bytes_accessed=4 * trunk_w2.size, transcendentals=0),
        name="load",
    )(*in_hbm(*small, branch_w))
    sums, w2_here = pl.pallas_call(
        functools.partial(group_kernel, row, nb * nq),
        out_shape=(
            jax.ShapeDtypeStruct((funcs, sums_width + early_width), BF),
            jax.ShapeDtypeStruct((hidden, width), BF),
        ),
        in_specs=[VMEM] * 7 + [HBM] * 2,
        out_specs=(VMEM,) * 2,
        scratch_shapes=[
            pltpu.VMEM((at_once, queries, hidden), BF),
            pltpu.VMEM(branch_w.shape, BF),
            pltpu.VMEM((2 * funcs, hidden), F32),
            pltpu.VMEM((2 * (dims + 1) * funcs, hidden), F32),
            pltpu.VMEM((funcs, queries), F32),
            pltpu.VMEM((at_once, 2 * (dims + 2) * funcs, queries), BF),
            pltpu.SemaphoreType.DMA((row - begun + 1,)),
        ],
        compiler_params=pltpu.CompilerParams(vmem_limit_bytes=40 * MIB),
        cost_estimate=pl.CostEstimate(
            flops=2 * 1024 * nq * queries * hidden, bytes_accessed=2 * branch_w.size, transcendentals=0
        ),
        name="group",
    )(got, got.transpose(1, 0, 2), *small, *in_hbm(branch_w, trunk_w2))

    def shift(x, k):
        return lax.ppermute(x, "branch", [(i, (i + k) % nb) for i in range(nb)])

    def swap(x):
        return lax.ppermute(x, "branch", [(i, i ^ 1) for i in range(nb)])

    if nb % 2:
        every = [sums] + [shift(sums, k) for k in range(1, nb)]
    else:
        every = [sums] + [shift(sums, k) for k in range(2, nb, 2)]
        every += [swap(x) for x in every]
    outs = (
        jax.ShapeDtypeStruct((branches, cut, width), F32),
        jax.ShapeDtypeStruct((branches, width), F32),
        jax.ShapeDtypeStruct((dims, hidden), F32),
        jax.ShapeDtypeStruct((1, hidden), F32),
        jax.ShapeDtypeStruct((hidden, width), F32),
        jax.ShapeDtypeStruct((1, width), F32),
    )
    gbw, gbb, gw1, gb1, gw2, gb2 = pl.pallas_call(
        functools.partial(tail_kernel, nb, early_width),
        out_shape=outs,
        in_specs=[VMEM] * (nb + 2),
        out_specs=(HBM,) * len(outs),
        scratch_shapes=[pltpu.VMEM(x.shape, F32) for x in outs]
        + [pltpu.SemaphoreType.DMA((BLOCKS + branches + 4,))],
        compiler_params=pltpu.CompilerParams(vmem_limit_bytes=24 * MIB),
        name="tail",
    )(*every, w2_here, small[1])
    return (gbw, gbb, gw1, gb1[0], gw2, gb2[0])


def solution(mesh):
    placed = (
        P(None, ("branch", "query"), None),
        P(),
        P(),
        P(None, ("branch", "query")),
        P(("branch", "query")),
        P(("branch", "query")),
        P(),
        P(),
        P(),
        P(),
    )
    return jax.shard_map(
        shards,
        mesh=mesh,
        in_specs=placed,
        out_specs=(P(None, "query", None), P(), P(), P(), P(), P()),
        check_vma=False,
    )
```

```python
import functools

import jax
import jax.numpy as jnp
from jax import lax
from jax.experimental import pallas as pl
from jax.experimental.pallas import tpu as pltpu
from jax.sharding import PartitionSpec as P

BF = jnp.bfloat16
F32 = jnp.float32
MIB = 1 << 20
VMEM = pl.BlockSpec(memory_space=pltpu.VMEM)
HBM = pl.BlockSpec(memory_space=pltpu.HBM)


def up(value, step):
    return -(-value // step) * step


def pieces(value, count):
    out = []
    for _ in range(count):
        top = value.astype(BF)
        out.append(top)
        value = value - top.astype(F32)
    return out


def dot(a, b, dims=((1,), (0,))):
    return lax.dot_general(a, b, (dims, ((), ())), preferred_element_type=F32)


def stack(rows, count):
    have = sum(r.shape[0] for r in rows)
    if have < count:
        rows = rows + [jnp.zeros((count - have, rows[0].shape[1]), rows[0].dtype)]
    return jnp.concatenate(rows, axis=0)


def in_hbm(*arrays):
    return [pltpu.with_memory_space_constraint(a, pltpu.HBM) for a in arrays]


def first_layer(w1_ref, b1_ref):
    rows = [w1_ref[...].astype(F32)] + [b.astype(F32) for b in pieces(b1_ref[...], 3)]
    return stack(rows, up(w1_ref.shape[0] + 3, 8)).astype(BF)


def hidden_units(xyz, first):
    a = stack([xyz, jnp.ones((3, xyz.shape[1]), F32)], first.shape[0]).T.astype(BF)
    return jnp.tanh(dot(a, first)).astype(BF)


def fetch(sems, first, *pairs):
    copies = [pltpu.make_async_copy(src, dst, sems.at[first + i]) for i, (src, dst) in enumerate(pairs)]
    for copy in copies:
        copy.start()
    return copies


def wait(copies):
    for copy in copies:
        copy.wait()


LANES = 128
BLOCKS = 8


def plan(branches, sensor_count, dims, q):
    lines = branches * sensor_count // q
    rows = up(-(-(lines + dims + 1) // 2), 8)
    return lines, rows, 2 * q + LANES * -(-(2 * q // LANES) // rows)


def line_of(block, i, q):
    return block[i // 2 : i // 2 + 1, i % 2 * q : (i % 2 + 1) * q]


def pack_kernel(sensors_hbm, coords_hbm, index_hbm, targets_hbm, out_ref, sensors_ref, coords_ref, index_ref, targets_ref, sems):
    wait(fetch(
        sems, 0, (sensors_hbm, sensors_ref), (coords_hbm, coords_ref), (index_hbm, index_ref), (targets_hbm, targets_ref)
    ))
    peers, rows, width = out_ref.shape
    q = coords_ref.shape[1]
    s, xyz = sensors_ref[...].astype(F32), coords_ref[...].astype(F32)
    lines = [s[k : k + 1, c : c + q] for k in range(s.shape[0]) for c in range(0, s.shape[1], q)]
    lines += [xyz[d : d + 1] for d in range(xyz.shape[0])] + [index_ref[...].astype(F32)]
    lines += [jnp.zeros((1, q), F32)] * (2 * rows - len(lines))
    main = jnp.concatenate([jnp.concatenate(lines[half::2], axis=0) for half in range(2)], axis=1)
    targets = jnp.concatenate([t.astype(F32) for t in pieces(targets_ref[...], 2)], axis=1)
    targets = [targets[:, c : c + LANES] for c in range(0, 2 * q, LANES)]
    beside = [stack(targets[c : c + rows], rows) for c in range(0, len(targets), rows)]
    block = jnp.concatenate([main] + beside, axis=1).astype(BF)
    for j in range(peers):
        out_ref[j] = block


def load_kernel(*refs):
    count = len(refs) // 2
    pairs = list(zip(refs[: count - 1], refs[count:-2]))
    w_hbm, begun_ref = refs[count - 1], refs[-2]
    blocks, q, _ = begun_ref.shape
    each = w_hbm.shape[1] // q
    pairs += [(w_hbm.at[i // each, pl.ds(i % each * q, q)], begun_ref.at[i]) for i in range(blocks)]
    wait(fetch(refs[-1], 0, *pairs))


def group_kernel(
    row, total_funcs,
    got_ref, turned_ref, bias_ref, b2_ref, w1_ref, b1_ref, begun_ref, w_hbm, w2_hbm,
    out_ref, w2_ref,
    h_ref, w_ref, g_ref, m_ref, r_ref, coef_ref, sems,
):
    chunks, rows, _ = got_ref.shape
    q = begun_ref.shape[1]
    funcs = turned_ref.shape[1]
    branches, sensor_count, width = w_ref.shape
    dims, hidden = w1_ref.shape
    cut = sensor_count // chunks
    scale = width ** (-0.5)
    at_once = h_ref.shape[0]
    ahead = at_once == chunks
    parts = [(k, c) for k in range(branches) for c in range(0, sensor_count, q)]
    begun = begun_ref.shape[0]
    copies = fetch(
        sems, 0, *[(w_hbm.at[k, pl.ds(c, q)], w_ref.at[k, pl.ds(c, q)]) for k, c in parts[begun:]], (w2_hbm, w2_ref)
    )

    pre = [bias_ref[k : k + 1, :] for k in range(branches)]

    def sensors(i):
        return turned_ref[i // 2, :, i % 2 * q : (i % 2 + 1) * q]

    def multiply(i):
        k, c = parts[i]
        if i < begun:
            block = begun_ref[i]
        else:
            copies[i - begun].wait()
            block = w_ref[k, c : c + q]
        pre[k] = pre[k] + dot(sensors(i), block)

    done = 0
    first = first_layer(w1_ref, b1_ref)

    def coords(block):
        return jnp.concatenate([line_of(block, row + d, q) for d in range(dims)], axis=0)

    def units(j):
        h_ref[j] = hidden_units(coords(got_ref[j].astype(F32)), first)

    held = 1 if ahead else 0
    if ahead:
        for j in range(chunks - held):
            units(j)
            ready = begun + (len(parts) - begun) * max(j - 1, 0) // chunks
            while done < ready:
                multiply(done)
                done += 1
    for i in range(done, len(parts)):
        multiply(i)
    for j in range(chunks - held, chunks if ahead else 0):
        units(j)
    lats = [jnp.tanh(p).astype(BF).astype(F32) for p in pre]
    product = (lats[0] * lats[1] * lats[2]).astype(BF)
    offset = jnp.sum(product.astype(F32) * b2_ref[...], axis=1, keepdims=True)
    copies[-1].wait()
    mixed_full = dot(product, w2_ref[...], ((1,), (1,)))
    mixed = jnp.concatenate(pieces(mixed_full, 2), axis=0)

    place = lax.broadcasted_iota(jnp.int32, (funcs, q), 0).astype(F32)
    one = jnp.ones((), BF)
    g_ref[...] = jnp.zeros_like(g_ref)
    m_ref[...] = jnp.zeros_like(m_ref)
    r_ref[...] = jnp.zeros_like(r_ref)

    def residuals(j, slot):
        block = got_ref[j].astype(F32)
        xyz = coords(block)
        owner = line_of(block, row + dims, q)
        target = [
            block[c % rows : c % rows + 1, 2 * q + c // rows * LANES : 2 * q + (c // rows + 1) * LANES]
            for c in range(2 * q // LANES)
        ]
        target = jnp.concatenate(target, axis=1)
        target = target[:, :q] + target[:, q:]
        if not ahead:
            h_ref[slot] = hidden_units(xyz, first)
        scores = dot(mixed, h_ref[slot], ((1,), (1,)))
        scores = scores[:funcs] + scores[funcs:] + offset
        owned = (owner == place).astype(F32)
        pred = jnp.sum(owned * scores, axis=0, keepdims=True) * scale
        resid = (pred - target) / total_funcs
        coef = owned * (resid * scale)
        spread = jnp.concatenate([coef] + [coef * xyz[d : d + 1] for d in range(dims)], axis=0)
        coef_ref[slot] = jnp.concatenate(pieces(coef, 2) + pieces(spread, 2), axis=0)
        return coef

    def batch(start):
        r = r_ref[...]
        for slot in range(at_once):
            r = r + residuals(start + slot, slot)
        r_ref[...] = r
        g, m = g_ref[...], m_ref[...]
        for slot in range(at_once):
            h = h_ref[slot]
            g = g + dot(coef_ref[slot, : 2 * funcs], h)
            m = m + dot(coef_ref[slot, 2 * funcs :], (one - h) * (one + h))
        g_ref[...] = g
        m_ref[...] = m

    if ahead:
        batch(0)
    else:
        lax.fori_loop(0, chunks // at_once, lambda i, carry: (batch(i * at_once), carry)[1], 0)

    r = jnp.broadcast_to(jnp.sum(r_ref[...], axis=1, keepdims=True), (funcs, LANES))
    high, low = pieces(r, 2)
    lane = lax.broadcasted_iota(jnp.int32, r.shape, 1)
    r = jnp.where(lane < LANES // 2, high.astype(F32), low.astype(F32))
    half = (dims + 1) * funcs
    moments = m_ref[:half] + m_ref[half:]
    extra = up(-(-(dims + 1) * hidden // funcs), LANES)
    grads = []
    for d in range(dims + 1):
        grad = jnp.sum(moments[d * funcs : (d + 1) * funcs] * mixed_full, axis=0, keepdims=True)
        grads += [grad[:, c : c + extra] for c in range(0, hidden, extra)]
    me = lax.axis_index("query")
    columns = []
    for k in range(branches):
        mine = jnp.zeros((funcs, cut), F32)
        for j in range(chunks):
            line, at = divmod(k * sensor_count + j * cut, q)
            mine = jnp.where(me == j, sensors(line)[:, at : at + cut].astype(F32), mine)
        columns.append(mine)
    flat = out_ref.shape[1] - width - LANES - extra - branches * width
    if flat > branches * cut:
        columns.append(jnp.zeros((funcs, flat - branches * cut), F32))
    sums = [g_ref[:funcs] + g_ref[funcs:], r, stack(grads, funcs)]
    out_ref[...] = jnp.concatenate(sums + lats + columns, axis=1).astype(BF)


def tail_kernel(groups, early_width, *refs):
    w2_ref, b2_ref = refs[groups : groups + 2]
    outs, bufs, sems = refs[groups + 2 : groups + 8], refs[groups + 8 : groups + 14], refs[-1]
    gbw_ref, gbb_ref, gw1_ref, gb1_ref, gw2_ref, gb2_ref = bufs
    width = w2_ref.shape[1]
    branches, cut, _ = gbw_ref.shape
    dims = gw1_ref.shape[0]
    all_rows = [x[...].astype(F32) for x in refs[:groups]]
    ends = all_rows[0].shape[1] - early_width
    copies = []

    def send(index, *at):
        source, target = bufs[index], outs[index]
        if at:
            source, target = source.at[at], target.at[at]
        copies.extend(fetch(sems, len(copies), (source, target)))

    def columns(first, count):
        return jnp.concatenate([x[:, first : first + count] for x in all_rows], axis=0)

    lat = [columns(ends + k * width, width) for k in range(branches)]
    product = (lat[0] * lat[1] * lat[2]).astype(BF)
    g = columns(0, width).astype(BF)
    height = gw2_ref.shape[0] // BLOCKS
    for c in range(0, gw2_ref.shape[0], height):
        gw2_ref[c : c + height] = dot(g[:, c : c + height], product, ((0,), (0,)))
        send(4, pl.ds(c, height))
    r = columns(width, LANES)
    r = r[:, :1] + r[:, LANES // 2 : LANES // 2 + 1]
    dprod = dot(g, w2_ref[...]) + r * b2_ref[...]
    lines = columns(ends + branches * width, branches * cut)
    gbb = []
    for k in range(branches):
        others = [lat[j] for j in range(branches) if j != k]
        delta = (dprod * (others[0] * others[1] * (1.0 - lat[k] * lat[k]))).astype(BF)
        gbw_ref[k] = dot(lines[:, k * cut : (k + 1) * cut].astype(BF), delta, ((0,), (0,)))
        send(0, k)
        gbb.append(jnp.sum(delta.astype(F32), axis=0, keepdims=True))
    gbb_ref[...] = jnp.concatenate(gbb, axis=0)
    parts = all_rows[0][:, width + LANES : ends]
    for x in all_rows[1:]:
        parts = parts + x[:, width + LANES : ends]
    each = gw1_ref.shape[1] // parts.shape[1]
    grads = [
        jnp.concatenate([parts[d * each + c : d * each + c + 1] for c in range(each)], axis=1) for d in range(dims + 1)
    ]
    gb1_ref[...] = grads[0]
    gw1_ref[...] = jnp.concatenate(grads[1:], axis=0)
    gb2_ref[...] = jnp.sum(r * product.astype(F32), axis=0, keepdims=True)
    for index in (1, 2, 3, 5):
        send(index)
    wait(copies)


def shards(
    sensors, branch_w, branch_b, coords, func_index, targets, trunk_w1, trunk_b1, trunk_w2, trunk_b2
):
    branches, func_dev, sensor_count = sensors.shape
    dims, queries = coords.shape
    hidden, width = trunk_w2.shape
    nb, nq = lax.axis_size("branch"), lax.axis_size("query")
    assert func_dev == 1 and hidden == width and sensor_count % queries == 0 and queries % (sensor_count // nq) == 0
    funcs = nq
    cut = sensor_count // nq
    row, rows, packed_width = plan(branches, sensor_count, dims, queries)
    at_once = nq if nq * queries * hidden * 2 <= 16 * MIB else 8
    assert nq % at_once == 0

    packed = pl.pallas_call(
        pack_kernel,
        out_shape=jax.ShapeDtypeStruct((nq, rows, packed_width), BF),
        in_specs=[HBM] * 4,
        out_specs=VMEM,
        scratch_shapes=[
            pltpu.VMEM((branches, sensor_count), BF),
            pltpu.VMEM((dims, queries), BF),
            pltpu.VMEM((1, queries), jnp.int32),
            pltpu.VMEM((1, queries), F32),
            pltpu.SemaphoreType.DMA((4,)),
        ],
        compiler_params=pltpu.CompilerParams(vmem_limit_bytes=8 * MIB),
        name="pack",
    )(*in_hbm(sensors.reshape(branches, sensor_count), coords, func_index[None], targets[None]))
    got = lax.all_to_all(packed, "query", 0, 0, tiled=True)

    early_width = branches * width + up(branches * cut, LANES)
    sums_width = width + LANES + up(-(-(dims + 1) * hidden // funcs), LANES)
    begun = min(row, 3 * MIB // (2 * queries * width))

    small = (branch_b, trunk_b2[None], trunk_w1, trunk_b1[None])
    shapes = [jax.ShapeDtypeStruct(x.shape, x.dtype) for x in small]
    small = pl.pallas_call(
        load_kernel,
        out_shape=(*shapes, jax.ShapeDtypeStruct((begun, queries, width), BF)),
        in_specs=[HBM] * (len(small) + 1),
        out_specs=(VMEM,) * (len(small) + 1),
        scratch_shapes=[pltpu.SemaphoreType.DMA((len(small) + begun,))],
        compiler_params=pltpu.CompilerParams(vmem_limit_bytes=8 * MIB),
        cost_estimate=pl.CostEstimate(flops=0, bytes_accessed=4 * trunk_w2.size, transcendentals=0),
        name="load",
    )(*in_hbm(*small, branch_w))
    sums, w2_here = pl.pallas_call(
        functools.partial(group_kernel, row, nb * nq),
        out_shape=(
            jax.ShapeDtypeStruct((funcs, sums_width + early_width), BF),
            jax.ShapeDtypeStruct((hidden, width), BF),
        ),
        in_specs=[VMEM] * 7 + [HBM] * 2,
        out_specs=(VMEM,) * 2,
        scratch_shapes=[
            pltpu.VMEM((at_once, queries, hidden), BF),
            pltpu.VMEM(branch_w.shape, BF),
            pltpu.VMEM((2 * funcs, hidden), F32),
            pltpu.VMEM((2 * (dims + 1) * funcs, hidden), F32),
            pltpu.VMEM((funcs, queries), F32),
            pltpu.VMEM((at_once, 2 * (dims + 2) * funcs, queries), BF),
            pltpu.SemaphoreType.DMA((row - begun + 1,)),
        ],
        compiler_params=pltpu.CompilerParams(vmem_limit_bytes=40 * MIB),
        cost_estimate=pl.CostEstimate(
            flops=2 * 1024 * nq * queries * hidden, bytes_accessed=2 * branch_w.size, transcendentals=0
        ),
        name="group",
    )(got, got.transpose(1, 0, 2), *small, *in_hbm(branch_w, trunk_w2))

    def shift(x, k):
        return lax.ppermute(x, "branch", [(i, (i + k) % nb) for i in range(nb)])

    def swap(x):
        return lax.ppermute(x, "branch", [(i, i ^ 1) for i in range(nb)])

    if nb % 2:
        every = [sums] + [shift(sums, k) for k in range(1, nb)]
    else:
        every = [sums] + [shift(sums, k) for k in range(2, nb, 2)]
        every += [swap(x) for x in every]
    outs = (
        jax.ShapeDtypeStruct((branches, cut, width), F32),
        jax.ShapeDtypeStruct((branches, width), F32),
        jax.ShapeDtypeStruct((dims, hidden), F32),
        jax.ShapeDtypeStruct((1, hidden), F32),
        jax.ShapeDtypeStruct((hidden, width), F32),
        jax.ShapeDtypeStruct((1, width), F32),
    )
    gbw, gbb, gw1, gb1, gw2, gb2 = pl.pallas_call(
        functools.partial(tail_kernel, nb, early_width),
        out_shape=outs,
        in_specs=[VMEM] * (nb + 2),
        out_specs=(HBM,) * len(outs),
        scratch_shapes=[pltpu.VMEM(x.shape, F32) for x in outs]
        + [pltpu.SemaphoreType.DMA((BLOCKS + branches + 4,))],
        compiler_params=pltpu.CompilerParams(vmem_limit_bytes=24 * MIB),
        name="tail",
    )(*every, w2_here, small[1])
    return (gbw, gbb, gw1, gb1[0], gw2, gb2[0])


def solution(mesh):
    placed = (
        P(None, ("branch", "query"), None),
        P(),
        P(),
        P(None, ("branch", "query")),
        P(("branch", "query")),
        P(("branch", "query")),
        P(),
        P(),
        P(),
        P(),
    )
    return jax.shard_map(
        shards,
        mesh=mesh,
        in_specs=placed,
        out_specs=(P(None, "query", None), P(), P(), P(), P(), P()),
        check_vma=False,
    )
```

```python
import functools

import jax
import jax.numpy as jnp
from jax import lax
from jax.experimental import pallas as pl
from jax.experimental.pallas import tpu as pltpu
from jax.sharding import PartitionSpec as P

BF = jnp.bfloat16
F32 = jnp.float32
MIB = 1 << 20
VMEM = pl.BlockSpec(memory_space=pltpu.VMEM)
HBM = pl.BlockSpec(memory_space=pltpu.HBM)


def up(value, step):
    return -(-value // step) * step


def pieces(value, count):
    out = []
    for _ in range(count):
        top = value.astype(BF)
        out.append(top)
        value = value - top.astype(F32)
    return out


def dot(a, b, dims=((1,), (0,))):
    return lax.dot_general(a, b, (dims, ((), ())), preferred_element_type=F32)


def stack(rows, count):
    have = sum(r.shape[0] for r in rows)
    if have < count:
        rows = rows + [jnp.zeros((count - have, rows[0].shape[1]), rows[0].dtype)]
    return jnp.concatenate(rows, axis=0)


def in_hbm(*arrays):
    return [pltpu.with_memory_space_constraint(a, pltpu.HBM) for a in arrays]


def first_layer(w1_ref, b1_ref):
    rows = [w1_ref[...].astype(F32)] + [b.astype(F32) for b in pieces(b1_ref[...], 3)]
    return stack(rows, up(w1_ref.shape[0] + 3, 8)).astype(BF)


def hidden_units(xyz, first):
    a = stack([xyz, jnp.ones((3, xyz.shape[1]), F32)], first.shape[0]).T.astype(BF)
    return jnp.tanh(dot(a, first)).astype(BF)


def fetch(sems, first, *pairs):
    copies = [pltpu.make_async_copy(src, dst, sems.at[first + i]) for i, (src, dst) in enumerate(pairs)]
    for copy in copies:
        copy.start()
    return copies


def wait(copies):
    for copy in copies:
        copy.wait()


LANES = 128
BLOCKS = 8


def plan(branches, sensor_count, dims, q):
    lines = branches * sensor_count // q
    rows = up(-(-(lines + dims + 1) // 2), 8)
    return lines, rows, 2 * q + LANES * -(-(2 * q // LANES) // rows)


def line_of(block, i, q):
    return block[i // 2 : i // 2 + 1, i % 2 * q : (i % 2 + 1) * q]


def pack_kernel(*refs):
    count = len(refs) // 2 - 1
    out_ref, (sensors_ref, coords_ref, index_ref, targets_ref, sems) = refs[count], refs[-5:]
    wait(fetch(sems, 0, *zip(refs[:4], refs[-5:-1]), *zip(refs[4:count], refs[count + 1 : -5])))
    peers, rows, width = out_ref.shape
    q = coords_ref.shape[1]
    s, xyz = sensors_ref[...].astype(F32), coords_ref[...].astype(F32)
    lines = [s[k : k + 1, c : c + q] for k in range(s.shape[0]) for c in range(0, s.shape[1], q)]
    lines += [xyz[d : d + 1] for d in range(xyz.shape[0])] + [index_ref[...].astype(F32)]
    lines += [jnp.zeros((1, q), F32)] * (2 * rows - len(lines))
    main = jnp.concatenate([jnp.concatenate(lines[half::2], axis=0) for half in range(2)], axis=1)
    targets = jnp.concatenate([t.astype(F32) for t in pieces(targets_ref[...], 2)], axis=1)
    targets = [targets[:, c : c + LANES] for c in range(0, 2 * q, LANES)]
    beside = [stack(targets[c : c + rows], rows) for c in range(0, len(targets), rows)]
    block = jnp.concatenate([main] + beside, axis=1).astype(BF)
    for j in range(peers):
        out_ref[j] = block


def group_kernel(
    row, total_funcs,
    got_ref, turned_ref, bias_ref, b2_ref, w1_ref, b1_ref, w_hbm, w2_hbm,
    out_ref, w2_ref,
    h_ref, w_ref, g_ref, m_ref, r_ref, coef_ref, sems,
):
    chunks, rows, _ = got_ref.shape
    q = h_ref.shape[1]
    funcs = turned_ref.shape[1]
    branches, sensor_count, width = w_ref.shape
    dims, hidden = w1_ref.shape
    cut = sensor_count // chunks
    scale = width ** (-0.5)
    at_once = h_ref.shape[0]
    ahead = at_once == chunks
    parts = [(k, c) for k in range(branches) for c in range(0, sensor_count, q)]
    copies = fetch(
        sems, 0, *[(w_hbm.at[k, pl.ds(c, q)], w_ref.at[k, pl.ds(c, q)]) for k, c in parts], (w2_hbm, w2_ref)
    )

    pre = [bias_ref[k : k + 1, :] for k in range(branches)]

    def sensors(i):
        return turned_ref[i // 2, :, i % 2 * q : (i % 2 + 1) * q]

    def multiply(i):
        k, c = parts[i]
        copies[i].wait()
        pre[k] = pre[k] + dot(sensors(i), w_ref[k, c : c + q])

    done = 0
    first = first_layer(w1_ref, b1_ref)

    def coords(block):
        return jnp.concatenate([line_of(block, row + d, q) for d in range(dims)], axis=0)

    def units(j):
        h_ref[j] = hidden_units(coords(got_ref[j].astype(F32)), first)

    held = 1 if ahead else 0
    if ahead:
        for j in range(chunks - held):
            units(j)
            ready = len(parts) * max(j - 1, 0) // chunks
            while done < ready:
                multiply(done)
                done += 1
    for i in range(done, len(parts)):
        multiply(i)
    for j in range(chunks - held, chunks if ahead else 0):
        units(j)
    lats = [jnp.tanh(p).astype(BF).astype(F32) for p in pre]
    product = (lats[0] * lats[1] * lats[2]).astype(BF)
    offset = jnp.sum(product.astype(F32) * b2_ref[...], axis=1, keepdims=True)
    copies[-1].wait()
    mixed_full = dot(product, w2_ref[...], ((1,), (1,)))
    mixed = jnp.concatenate(pieces(mixed_full, 2), axis=0)

    place = lax.broadcasted_iota(jnp.int32, (funcs, q), 0).astype(F32)
    one = jnp.ones((), BF)
    g_ref[...] = jnp.zeros_like(g_ref)
    m_ref[...] = jnp.zeros_like(m_ref)
    r_ref[...] = jnp.zeros_like(r_ref)

    def residuals(j, slot):
        block = got_ref[j].astype(F32)
        xyz = coords(block)
        owner = line_of(block, row + dims, q)
        target = [
            block[c % rows : c % rows + 1, 2 * q + c // rows * LANES : 2 * q + (c // rows + 1) * LANES]
            for c in range(2 * q // LANES)
        ]
        target = jnp.concatenate(target, axis=1)
        target = target[:, :q] + target[:, q:]
        if not ahead:
            h_ref[slot] = hidden_units(xyz, first)
        scores = dot(mixed, h_ref[slot], ((1,), (1,)))
        scores = scores[:funcs] + scores[funcs:] + offset
        owned = (owner == place).astype(F32)
        pred = jnp.sum(owned * scores, axis=0, keepdims=True) * scale
        resid = (pred - target) / total_funcs
        coef = owned * (resid * scale)
        spread = jnp.concatenate([coef] + [coef * xyz[d : d + 1] for d in range(dims)], axis=0)
        coef_ref[slot] = jnp.concatenate(pieces(coef, 2) + pieces(spread, 2), axis=0)
        return coef

    def batch(start):
        r = r_ref[...]
        for slot in range(at_once):
            r = r + residuals(start + slot, slot)
        r_ref[...] = r
        g, m = g_ref[...], m_ref[...]
        for slot in range(at_once):
            h = h_ref[slot]
            g = g + dot(coef_ref[slot, : 2 * funcs], h)
            m = m + dot(coef_ref[slot, 2 * funcs :], (one - h) * (one + h))
        g_ref[...] = g
        m_ref[...] = m

    if ahead:
        batch(0)
    else:
        lax.fori_loop(0, chunks // at_once, lambda i, carry: (batch(i * at_once), carry)[1], 0)

    r = jnp.broadcast_to(jnp.sum(r_ref[...], axis=1, keepdims=True), (funcs, LANES))
    high, low = pieces(r, 2)
    lane = lax.broadcasted_iota(jnp.int32, r.shape, 1)
    r = jnp.where(lane < LANES // 2, high.astype(F32), low.astype(F32))
    half = (dims + 1) * funcs
    moments = m_ref[:half] + m_ref[half:]
    extra = up(-(-(dims + 1) * hidden // funcs), LANES)
    grads = []
    for d in range(dims + 1):
        grad = jnp.sum(moments[d * funcs : (d + 1) * funcs] * mixed_full, axis=0, keepdims=True)
        grads += [grad[:, c : c + extra] for c in range(0, hidden, extra)]
    me = lax.axis_index("query")
    columns = []
    for k in range(branches):
        mine = jnp.zeros((funcs, cut), F32)
        for j in range(chunks):
            line, at = divmod(k * sensor_count + j * cut, q)
            mine = jnp.where(me == j, sensors(line)[:, at : at + cut].astype(F32), mine)
        columns.append(mine)
    flat = out_ref.shape[1] - width - LANES - extra - branches * width
    if flat > branches * cut:
        columns.append(jnp.zeros((funcs, flat - branches * cut), F32))
    sums = [g_ref[:funcs] + g_ref[funcs:], r, stack(grads, funcs)]
    out_ref[...] = jnp.concatenate(sums + lats + columns, axis=1).astype(BF)


def tail_kernel(groups, early_width, *refs):
    w2_ref, b2_ref = refs[groups : groups + 2]
    outs, bufs, sems = refs[groups + 2 : groups + 8], refs[groups + 8 : groups + 14], refs[-1]
    gbw_ref, gbb_ref, gw1_ref, gb1_ref, gw2_ref, gb2_ref = bufs
    width = w2_ref.shape[1]
    branches, cut, _ = gbw_ref.shape
    dims = gw1_ref.shape[0]
    all_rows = [x[...].astype(F32) for x in refs[:groups]]
    ends = all_rows[0].shape[1] - early_width
    copies = []

    def send(index, *at):
        source, target = bufs[index], outs[index]
        if at:
            source, target = source.at[at], target.at[at]
        copies.extend(fetch(sems, len(copies), (source, target)))

    def columns(first, count):
        return jnp.concatenate([x[:, first : first + count] for x in all_rows], axis=0)

    lat = [columns(ends + k * width, width) for k in range(branches)]
    product = (lat[0] * lat[1] * lat[2]).astype(BF)
    g = columns(0, width).astype(BF)
    height = gw2_ref.shape[0] // BLOCKS
    for c in range(0, gw2_ref.shape[0], height):
        gw2_ref[c : c + height] = dot(g[:, c : c + height], product, ((0,), (0,)))
        send(4, pl.ds(c, height))
    r = columns(width, LANES)
    r = r[:, :1] + r[:, LANES // 2 : LANES // 2 + 1]
    dprod = dot(g, w2_ref[...]) + r * b2_ref[...]
    lines = columns(ends + branches * width, branches * cut)
    gbb = []
    for k in range(branches):
        others = [lat[j] for j in range(branches) if j != k]
        delta = (dprod * (others[0] * others[1] * (1.0 - lat[k] * lat[k]))).astype(BF)
        gbw_ref[k] = dot(lines[:, k * cut : (k + 1) * cut].astype(BF), delta, ((0,), (0,)))
        send(0, k)
        gbb.append(jnp.sum(delta.astype(F32), axis=0, keepdims=True))
    gbb_ref[...] = jnp.concatenate(gbb, axis=0)
    parts = all_rows[0][:, width + LANES : ends]
    for x in all_rows[1:]:
        parts = parts + x[:, width + LANES : ends]
    each = gw1_ref.shape[1] // parts.shape[1]
    grads = [
        jnp.concatenate([parts[d * each + c : d * each + c + 1] for c in range(each)], axis=1) for d in range(dims + 1)
    ]
    gb1_ref[...] = grads[0]
    gw1_ref[...] = jnp.concatenate(grads[1:], axis=0)
    gb2_ref[...] = jnp.sum(r * product.astype(F32), axis=0, keepdims=True)
    for index in (1, 2, 3, 5):
        send(index)
    wait(copies)


def shards(
    sensors, branch_w, branch_b, coords, func_index, targets, trunk_w1, trunk_b1, trunk_w2, trunk_b2
):
    branches, func_dev, sensor_count = sensors.shape
    dims, queries = coords.shape
    hidden, width = trunk_w2.shape
    nb, nq = lax.axis_size("branch"), lax.axis_size("query")
    assert func_dev == 1 and hidden == width and sensor_count % queries == 0 and queries % (sensor_count // nq) == 0
    funcs = nq
    cut = sensor_count // nq
    row, rows, packed_width = plan(branches, sensor_count, dims, queries)
    at_once = nq if nq * queries * hidden * 2 <= 16 * MIB else 8
    assert nq % at_once == 0

    small = (branch_b, trunk_b2[None], trunk_w1, trunk_b1[None])
    packed, *small_here = pl.pallas_call(
        pack_kernel,
        out_shape=(
            jax.ShapeDtypeStruct((nq, rows, packed_width), BF),
            *[jax.ShapeDtypeStruct(x.shape, x.dtype) for x in small],
        ),
        in_specs=[HBM] * (4 + len(small)),
        out_specs=(VMEM,) * (1 + len(small)),
        scratch_shapes=[
            pltpu.VMEM((branches, sensor_count), BF),
            pltpu.VMEM((dims, queries), BF),
            pltpu.VMEM((1, queries), jnp.int32),
            pltpu.VMEM((1, queries), F32),
            pltpu.SemaphoreType.DMA((4 + len(small),)),
        ],
        compiler_params=pltpu.CompilerParams(vmem_limit_bytes=8 * MIB),
        name="pack",
    )(*in_hbm(sensors.reshape(branches, sensor_count), coords, func_index[None], targets[None], *small))
    got = lax.all_to_all(packed, "query", 0, 0, tiled=True)

    early_width = branches * width + up(branches * cut, LANES)
    sums_width = width + LANES + up(-(-(dims + 1) * hidden // funcs), LANES)
    sums, w2_here = pl.pallas_call(
        functools.partial(group_kernel, row, nb * nq),
        out_shape=(
            jax.ShapeDtypeStruct((funcs, sums_width + early_width), BF),
            jax.ShapeDtypeStruct((hidden, width), BF),
        ),
        in_specs=[VMEM] * 6 + [HBM] * 2,
        out_specs=(VMEM,) * 2,
        scratch_shapes=[
            pltpu.VMEM((at_once, queries, hidden), BF),
            pltpu.VMEM(branch_w.shape, BF),
            pltpu.VMEM((2 * funcs, hidden), F32),
            pltpu.VMEM((2 * (dims + 1) * funcs, hidden), F32),
            pltpu.VMEM((funcs, queries), F32),
            pltpu.VMEM((at_once, 2 * (dims + 2) * funcs, queries), BF),
            pltpu.SemaphoreType.DMA((row + 1,)),
        ],
        compiler_params=pltpu.CompilerParams(vmem_limit_bytes=40 * MIB),
        cost_estimate=pl.CostEstimate(
            flops=2 * 1024 * nq * queries * hidden, bytes_accessed=2 * branch_w.size, transcendentals=0
        ),
        name="group",
    )(got, got.transpose(1, 0, 2), *small_here, *in_hbm(branch_w, trunk_w2))

    def shift(x, k):
        return lax.ppermute(x, "branch", [(i, (i + k) % nb) for i in range(nb)])

    def swap(x):
        return lax.ppermute(x, "branch", [(i, i ^ 1) for i in range(nb)])

    if nb % 2:
        every = [sums] + [shift(sums, k) for k in range(1, nb)]
    else:
        every = [sums] + [shift(sums, k) for k in range(2, nb, 2)]
        every += [swap(x) for x in every]
    outs = (
        jax.ShapeDtypeStruct((branches, cut, width), F32),
        jax.ShapeDtypeStruct((branches, width), F32),
        jax.ShapeDtypeStruct((dims, hidden), F32),
        jax.ShapeDtypeStruct((1, hidden), F32),
        jax.ShapeDtypeStruct((hidden, width), F32),
        jax.ShapeDtypeStruct((1, width), F32),
    )
    gbw, gbb, gw1, gb1, gw2, gb2 = pl.pallas_call(
        functools.partial(tail_kernel, nb, early_width),
        out_shape=outs,
        in_specs=[VMEM] * (nb + 2),
        out_specs=(HBM,) * len(outs),
        scratch_shapes=[pltpu.VMEM(x.shape, F32) for x in outs]
        + [pltpu.SemaphoreType.DMA((BLOCKS + branches + 4,))],
        compiler_params=pltpu.CompilerParams(vmem_limit_bytes=24 * MIB),
        name="tail",
    )(*every, w2_here, small_here[1])
    return (gbw, gbb, gw1, gb1[0], gw2, gb2[0])


def solution(mesh):
    placed = (
        P(None, ("branch", "query"), None),
        P(),
        P(),
        P(None, ("branch", "query")),
        P(("branch", "query")),
        P(("branch", "query")),
        P(),
        P(),
        P(),
        P(),
    )
    return jax.shard_map(
        shards,
        mesh=mesh,
        in_specs=placed,
        out_specs=(P(None, "query", None), P(), P(), P(), P(), P()),
        check_vma=False,
    )
```

```python
import functools

import jax
import jax.numpy as jnp
from jax import lax
from jax.experimental import pallas as pl
from jax.experimental.pallas import tpu as pltpu
from jax.sharding import PartitionSpec as P

BF = jnp.bfloat16
F32 = jnp.float32
MIB = 1 << 20
VMEM = pl.BlockSpec(memory_space=pltpu.VMEM)
HBM = pl.BlockSpec(memory_space=pltpu.HBM)


def up(value, step):
    return -(-value // step) * step


def pieces(value, count):
    out = []
    for _ in range(count):
        top = value.astype(BF)
        out.append(top)
        value = value - top.astype(F32)
    return out


def dot(a, b, dims=((1,), (0,))):
    return lax.dot_general(a, b, (dims, ((), ())), preferred_element_type=F32)


def stack(rows, count):
    have = sum(r.shape[0] for r in rows)
    if have < count:
        rows = rows + [jnp.zeros((count - have, rows[0].shape[1]), rows[0].dtype)]
    return jnp.concatenate(rows, axis=0)


def in_hbm(*arrays):
    return [pltpu.with_memory_space_constraint(a, pltpu.HBM) for a in arrays]


def first_layer(w1_ref, b1_ref):
    rows = [w1_ref[...].astype(F32)] + [b.astype(F32) for b in pieces(b1_ref[...], 3)]
    return stack(rows, up(w1_ref.shape[0] + 3, 8)).astype(BF)


def hidden_units(xyz, first):
    a = stack([xyz, jnp.ones((3, xyz.shape[1]), F32)], first.shape[0]).T.astype(BF)
    return jnp.tanh(dot(a, first)).astype(BF)


def fetch(sems, first, *pairs):
    copies = [pltpu.make_async_copy(src, dst, sems.at[first + i]) for i, (src, dst) in enumerate(pairs)]
    for copy in copies:
        copy.start()
    return copies


def wait(copies):
    for copy in copies:
        copy.wait()


LANES = 128
BLOCKS = 8


def plan(branches, sensor_count, dims, q):
    lines = branches * sensor_count // q
    rows = up(-(-(lines + dims + 1) // 2), 8)
    return lines, rows, 2 * q + LANES * -(-(2 * q // LANES) // rows)


def line_of(block, i, q):
    return block[i // 2 : i // 2 + 1, i % 2 * q : (i % 2 + 1) * q]


def pack_kernel(*refs):
    count = len(refs) // 2 - 1
    out_ref, (sensors_ref, coords_ref, index_ref, targets_ref, sems) = refs[count], refs[-5:]
    wait(fetch(sems, 0, *zip(refs[:4], refs[-5:-1]), *zip(refs[4:count], refs[count + 1 : -5])))
    peers, rows, width = out_ref.shape
    q = coords_ref.shape[1]
    s, xyz = sensors_ref[...].astype(F32), coords_ref[...].astype(F32)
    lines = [s[k : k + 1, c : c + q] for k in range(s.shape[0]) for c in range(0, s.shape[1], q)]
    lines += [xyz[d : d + 1] for d in range(xyz.shape[0])] + [index_ref[...].astype(F32)]
    lines += [jnp.zeros((1, q), F32)] * (2 * rows - len(lines))
    main = jnp.concatenate([jnp.concatenate(lines[half::2], axis=0) for half in range(2)], axis=1)
    targets = jnp.concatenate([t.astype(F32) for t in pieces(targets_ref[...], 2)], axis=1)
    targets = [targets[:, c : c + LANES] for c in range(0, 2 * q, LANES)]
    beside = [stack(targets[c : c + rows], rows) for c in range(0, len(targets), rows)]
    block = jnp.concatenate([main] + beside, axis=1).astype(BF)
    for j in range(peers):
        out_ref[j] = block


def group_kernel(
    row, total_funcs,
    got_ref, turned_ref, bias_ref, b2_ref, w1_ref, b1_ref, w_hbm, w2_hbm,
    out_ref, w2_ref,
    h_ref, w_ref, g_ref, m_ref, r_ref, coef_ref, sems,
):
    chunks, rows, _ = got_ref.shape
    q = h_ref.shape[1]
    funcs = turned_ref.shape[1]
    branches, sensor_count, width = w_ref.shape
    dims, hidden = w1_ref.shape
    cut = sensor_count // chunks
    scale = width ** (-0.5)
    at_once = h_ref.shape[0]
    ahead = at_once == chunks
    parts = [(k, c) for k in range(branches) for c in range(0, sensor_count, 2 * q)]
    copies = fetch(
        sems, 0, *[(w_hbm.at[k, pl.ds(c, 2 * q)], w_ref.at[k, pl.ds(c, 2 * q)]) for k, c in parts], (w2_hbm, w2_ref)
    )

    pre = [bias_ref[k : k + 1, :] for k in range(branches)]

    def sensors(i):
        return turned_ref[i // 2, :, i % 2 * q : (i % 2 + 1) * q]

    def multiply(i):
        k, c = parts[i]
        copies[i].wait()
        pre[k] = pre[k] + dot(turned_ref[i, :, : 2 * q], w_ref[k, c : c + 2 * q])

    done = 0
    first = first_layer(w1_ref, b1_ref)

    def coords(block):
        return jnp.concatenate([line_of(block, row + d, q) for d in range(dims)], axis=0)

    def units(j):
        h_ref[j] = hidden_units(coords(got_ref[j].astype(F32)), first)

    held = 1 if ahead else 0
    if ahead:
        for j in range(chunks - held):
            units(j)
            ready = len(parts) * max(j - 1, 0) // chunks
            while done < ready:
                multiply(done)
                done += 1
    for i in range(done, len(parts)):
        multiply(i)
    for j in range(chunks - held, chunks if ahead else 0):
        units(j)
    lats = [jnp.tanh(p).astype(BF).astype(F32) for p in pre]
    product = (lats[0] * lats[1] * lats[2]).astype(BF)
    offset = jnp.sum(product.astype(F32) * b2_ref[...], axis=1, keepdims=True)
    copies[-1].wait()
    mixed_full = dot(product, w2_ref[...], ((1,), (1,)))
    mixed = jnp.concatenate(pieces(mixed_full, 2), axis=0)

    place = lax.broadcasted_iota(jnp.int32, (funcs, q), 0).astype(F32)
    one = jnp.ones((), BF)
    g_ref[...] = jnp.zeros_like(g_ref)
    m_ref[...] = jnp.zeros_like(m_ref)
    r_ref[...] = jnp.zeros_like(r_ref)

    def residuals(j, slot):
        block = got_ref[j].astype(F32)
        xyz = coords(block)
        owner = line_of(block, row + dims, q)
        target = [
            block[c % rows : c % rows + 1, 2 * q + c // rows * LANES : 2 * q + (c // rows + 1) * LANES]
            for c in range(2 * q // LANES)
        ]
        target = jnp.concatenate(target, axis=1)
        target = target[:, :q] + target[:, q:]
        if not ahead:
            h_ref[slot] = hidden_units(xyz, first)
        scores = dot(mixed, h_ref[slot], ((1,), (1,)))
        scores = scores[:funcs] + scores[funcs:] + offset
        owned = (owner == place).astype(F32)
        pred = jnp.sum(owned * scores, axis=0, keepdims=True) * scale
        resid = (pred - target) / total_funcs
        coef = owned * (resid * scale)
        spread = jnp.concatenate([coef] + [coef * xyz[d : d + 1] for d in range(dims)], axis=0)
        coef_ref[slot] = jnp.concatenate(pieces(coef, 2) + pieces(spread, 2), axis=0)
        return coef

    def batch(start):
        r = r_ref[...]
        for slot in range(at_once):
            r = r + residuals(start + slot, slot)
        r_ref[...] = r
        g, m = g_ref[...], m_ref[...]
        for slot in range(at_once):
            h = h_ref[slot]
            g = g + dot(coef_ref[slot, : 2 * funcs], h)
            m = m + dot(coef_ref[slot, 2 * funcs :], (one - h) * (one + h))
        g_ref[...] = g
        m_ref[...] = m

    if ahead:
        batch(0)
    else:
        lax.fori_loop(0, chunks // at_once, lambda i, carry: (batch(i * at_once), carry)[1], 0)

    r = jnp.broadcast_to(jnp.sum(r_ref[...], axis=1, keepdims=True), (funcs, LANES))
    high, low = pieces(r, 2)
    lane = lax.broadcasted_iota(jnp.int32, r.shape, 1)
    r = jnp.where(lane < LANES // 2, high.astype(F32), low.astype(F32))
    half = (dims + 1) * funcs
    moments = m_ref[:half] + m_ref[half:]
    extra = up(-(-(dims + 1) * hidden // funcs), LANES)
    grads = []
    for d in range(dims + 1):
        grad = jnp.sum(moments[d * funcs : (d + 1) * funcs] * mixed_full, axis=0, keepdims=True)
        grads += [grad[:, c : c + extra] for c in range(0, hidden, extra)]
    me = lax.axis_index("query")
    columns = []
    for k in range(branches):
        mine = jnp.zeros((funcs, cut), F32)
        for j in range(chunks):
            line, at = divmod(k * sensor_count + j * cut, q)
            mine = jnp.where(me == j, sensors(line)[:, at : at + cut].astype(F32), mine)
        columns.append(mine)
    flat = out_ref.shape[1] - width - LANES - extra - branches * width
    if flat > branches * cut:
        columns.append(jnp.zeros((funcs, flat - branches * cut), F32))
    sums = [g_ref[:funcs] + g_ref[funcs:], r, stack(grads, funcs)]
    out_ref[...] = jnp.concatenate(sums + lats + columns, axis=1).astype(BF)


def tail_kernel(groups, early_width, *refs):
    w2_ref, b2_ref = refs[groups : groups + 2]
    outs, bufs, sems = refs[groups + 2 : groups + 8], refs[groups + 8 : groups + 14], refs[-1]
    gbw_ref, gbb_ref, gw1_ref, gb1_ref, gw2_ref, gb2_ref = bufs
    width = w2_ref.shape[1]
    branches, cut, _ = gbw_ref.shape
    dims = gw1_ref.shape[0]
    all_rows = [x[...].astype(F32) for x in refs[:groups]]
    ends = all_rows[0].shape[1] - early_width
    copies = []

    def send(index, *at):
        source, target = bufs[index], outs[index]
        if at:
            source, target = source.at[at], target.at[at]
        copies.extend(fetch(sems, len(copies), (source, target)))

    def columns(first, count):
        return jnp.concatenate([x[:, first : first + count] for x in all_rows], axis=0)

    lat = [columns(ends + k * width, width) for k in range(branches)]
    product = (lat[0] * lat[1] * lat[2]).astype(BF)
    g = columns(0, width).astype(BF)
    height = gw2_ref.shape[0] // BLOCKS
    for c in range(0, gw2_ref.shape[0], height):
        gw2_ref[c : c + height] = dot(g[:, c : c + height], product, ((0,), (0,)))
        send(4, pl.ds(c, height))
    r = columns(width, LANES)
    r = r[:, :1] + r[:, LANES // 2 : LANES // 2 + 1]
    dprod = dot(g, w2_ref[...]) + r * b2_ref[...]
    lines = columns(ends + branches * width, branches * cut)
    gbb = []
    for k in range(branches):
        others = [lat[j] for j in range(branches) if j != k]
        delta = (dprod * (others[0] * others[1] * (1.0 - lat[k] * lat[k]))).astype(BF)
        gbw_ref[k] = dot(lines[:, k * cut : (k + 1) * cut].astype(BF), delta, ((0,), (0,)))
        send(0, k)
        gbb.append(jnp.sum(delta.astype(F32), axis=0, keepdims=True))
    gbb_ref[...] = jnp.concatenate(gbb, axis=0)
    parts = all_rows[0][:, width + LANES : ends]
    for x in all_rows[1:]:
        parts = parts + x[:, width + LANES : ends]
    each = gw1_ref.shape[1] // parts.shape[1]
    grads = [
        jnp.concatenate([parts[d * each + c : d * each + c + 1] for c in range(each)], axis=1) for d in range(dims + 1)
    ]
    gb1_ref[...] = grads[0]
    gw1_ref[...] = jnp.concatenate(grads[1:], axis=0)
    gb2_ref[...] = jnp.sum(r * product.astype(F32), axis=0, keepdims=True)
    for index in (1, 2, 3, 5):
        send(index)
    wait(copies)


def shards(
    sensors, branch_w, branch_b, coords, func_index, targets, trunk_w1, trunk_b1, trunk_w2, trunk_b2
):
    branches, func_dev, sensor_count = sensors.shape
    dims, queries = coords.shape
    hidden, width = trunk_w2.shape
    nb, nq = lax.axis_size("branch"), lax.axis_size("query")
    assert func_dev == 1 and hidden == width and sensor_count % (2 * queries) == 0 and queries % (sensor_count // nq) == 0
    funcs = nq
    cut = sensor_count // nq
    row, rows, packed_width = plan(branches, sensor_count, dims, queries)
    at_once = nq if nq * queries * hidden * 2 <= 16 * MIB else 8
    assert nq % at_once == 0

    small = (branch_b, trunk_b2[None], trunk_w1, trunk_b1[None])
    packed, *small_here = pl.pallas_call(
        pack_kernel,
        out_shape=(
            jax.ShapeDtypeStruct((nq, rows, packed_width), BF),
            *[jax.ShapeDtypeStruct(x.shape, x.dtype) for x in small],
        ),
        in_specs=[HBM] * (4 + len(small)),
        out_specs=(VMEM,) * (1 + len(small)),
        scratch_shapes=[
            pltpu.VMEM((branches, sensor_count), BF),
            pltpu.VMEM((dims, queries), BF),
            pltpu.VMEM((1, queries), jnp.int32),
            pltpu.VMEM((1, queries), F32),
            pltpu.SemaphoreType.DMA((4 + len(small),)),
        ],
        compiler_params=pltpu.CompilerParams(vmem_limit_bytes=8 * MIB),
        name="pack",
    )(*in_hbm(sensors.reshape(branches, sensor_count), coords, func_index[None], targets[None], *small))
    got = lax.all_to_all(packed, "query", 0, 0, tiled=True)

    early_width = branches * width + up(branches * cut, LANES)
    sums_width = width + LANES + up(-(-(dims + 1) * hidden // funcs), LANES)
    sums, w2_here = pl.pallas_call(
        functools.partial(group_kernel, row, nb * nq),
        out_shape=(
            jax.ShapeDtypeStruct((funcs, sums_width + early_width), BF),
            jax.ShapeDtypeStruct((hidden, width), BF),
        ),
        in_specs=[VMEM] * 6 + [HBM] * 2,
        out_specs=(VMEM,) * 2,
        scratch_shapes=[
            pltpu.VMEM((at_once, queries, hidden), BF),
            pltpu.VMEM(branch_w.shape, BF),
            pltpu.VMEM((2 * funcs, hidden), F32),
            pltpu.VMEM((2 * (dims + 1) * funcs, hidden), F32),
            pltpu.VMEM((funcs, queries), F32),
            pltpu.VMEM((at_once, 2 * (dims + 2) * funcs, queries), BF),
            pltpu.SemaphoreType.DMA((row // 2 + 1,)),
        ],
        compiler_params=pltpu.CompilerParams(vmem_limit_bytes=40 * MIB),
        cost_estimate=pl.CostEstimate(
            flops=2 * 1024 * nq * queries * hidden, bytes_accessed=2 * branch_w.size, transcendentals=0
        ),
        name="group",
    )(got, got.transpose(1, 0, 2), *small_here, *in_hbm(branch_w, trunk_w2))

    def shift(x, k):
        return lax.ppermute(x, "branch", [(i, (i + k) % nb) for i in range(nb)])

    def swap(x):
        return lax.ppermute(x, "branch", [(i, i ^ 1) for i in range(nb)])

    if nb % 2:
        every = [sums] + [shift(sums, k) for k in range(1, nb)]
    else:
        every = [sums] + [shift(sums, k) for k in range(2, nb, 2)]
        every += [swap(x) for x in every]
    outs = (
        jax.ShapeDtypeStruct((branches, cut, width), F32),
        jax.ShapeDtypeStruct((branches, width), F32),
        jax.ShapeDtypeStruct((dims, hidden), F32),
        jax.ShapeDtypeStruct((1, hidden), F32),
        jax.ShapeDtypeStruct((hidden, width), F32),
        jax.ShapeDtypeStruct((1, width), F32),
    )
    gbw, gbb, gw1, gb1, gw2, gb2 = pl.pallas_call(
        functools.partial(tail_kernel, nb, early_width),
        out_shape=outs,
        in_specs=[VMEM] * (nb + 2),
        out_specs=(HBM,) * len(outs),
        scratch_shapes=[pltpu.VMEM(x.shape, F32) for x in outs]
        + [pltpu.SemaphoreType.DMA((BLOCKS + branches + 4,))],
        compiler_params=pltpu.CompilerParams(vmem_limit_bytes=24 * MIB),
        name="tail",
    )(*every, w2_here, small_here[1])
    return (gbw, gbb, gw1, gb1[0], gw2, gb2[0])


def solution(mesh):
    placed = (
        P(None, ("branch", "query"), None),
        P(),
        P(),
        P(None, ("branch", "query")),
        P(("branch", "query")),
        P(("branch", "query")),
        P(),
        P(),
        P(),
        P(),
    )
    return jax.shard_map(
        shards,
        mesh=mesh,
        in_specs=placed,
        out_specs=(P(None, "query", None), P(), P(), P(), P(), P()),
        check_vma=False,
    )
```

```python
import functools

import jax
import jax.numpy as jnp
from jax import lax
from jax.experimental import pallas as pl
from jax.experimental.pallas import tpu as pltpu
from jax.sharding import PartitionSpec as P

BF = jnp.bfloat16
F32 = jnp.float32
MIB = 1 << 20
VMEM = pl.BlockSpec(memory_space=pltpu.VMEM)
HBM = pl.BlockSpec(memory_space=pltpu.HBM)


def up(value, step):
    return -(-value // step) * step


def pieces(value, count):
    out = []
    for _ in range(count):
        top = value.astype(BF)
        out.append(top)
        value = value - top.astype(F32)
    return out


def dot(a, b, dims=((1,), (0,))):
    return lax.dot_general(a, b, (dims, ((), ())), preferred_element_type=F32)


def stack(rows, count):
    have = sum(r.shape[0] for r in rows)
    if have < count:
        rows = rows + [jnp.zeros((count - have, rows[0].shape[1]), rows[0].dtype)]
    return jnp.concatenate(rows, axis=0)


def in_hbm(*arrays):
    return [pltpu.with_memory_space_constraint(a, pltpu.HBM) for a in arrays]


def first_layer(w1_ref, b1_ref):
    rows = [w1_ref[...].astype(F32)] + [b.astype(F32) for b in pieces(b1_ref[...], 3)]
    return stack(rows, up(w1_ref.shape[0] + 3, 8)).astype(BF)


def hidden_units(xyz, first):
    a = stack([xyz, jnp.ones((3, xyz.shape[1]), F32)], first.shape[0]).T.astype(BF)
    return jnp.tanh(dot(a, first)).astype(BF)


def fetch(sems, first, *pairs):
    copies = [pltpu.make_async_copy(src, dst, sems.at[first + i]) for i, (src, dst) in enumerate(pairs)]
    for copy in copies:
        copy.start()
    return copies


def wait(copies):
    for copy in copies:
        copy.wait()


LANES = 128
BLOCKS = 4


def plan(branches, sensor_count, dims, q):
    lines = branches * sensor_count // q
    rows = up(-(-(lines + dims + 1) // 2), 8)
    return lines, rows, 2 * q + LANES * -(-(2 * q // LANES) // rows)


def line_of(block, i, q):
    return block[i // 2 : i // 2 + 1, i % 2 * q : (i % 2 + 1) * q]


def pack_kernel(*refs):
    count = len(refs) // 2 - 1
    out_ref, (sensors_ref, coords_ref, index_ref, targets_ref, sems) = refs[count], refs[-5:]
    wait(fetch(sems, 0, *zip(refs[:4], refs[-5:-1]), *zip(refs[4:count], refs[count + 1 : -5])))
    peers, rows, width = out_ref.shape
    q = coords_ref.shape[1]
    s, xyz = sensors_ref[...].astype(F32), coords_ref[...].astype(F32)
    lines = [s[k : k + 1, c : c + q] for k in range(s.shape[0]) for c in range(0, s.shape[1], q)]
    lines += [xyz[d : d + 1] for d in range(xyz.shape[0])] + [index_ref[...].astype(F32)]
    lines += [jnp.zeros((1, q), F32)] * (2 * rows - len(lines))
    main = jnp.concatenate([jnp.concatenate(lines[half::2], axis=0) for half in range(2)], axis=1)
    targets = jnp.concatenate([t.astype(F32) for t in pieces(targets_ref[...], 2)], axis=1)
    targets = [targets[:, c : c + LANES] for c in range(0, 2 * q, LANES)]
    beside = [stack(targets[c : c + rows], rows) for c in range(0, len(targets), rows)]
    block = jnp.concatenate([main] + beside, axis=1).astype(BF)
    for j in range(peers):
        out_ref[j] = block


def group_kernel(
    row, total_funcs,
    got_ref, turned_ref, bias_ref, b2_ref, w1_ref, b1_ref, w_hbm, w2_hbm,
    out_ref, w2_ref,
    h_ref, w_ref, g_ref, m_ref, r_ref, coef_ref, sems,
):
    chunks, rows, _ = got_ref.shape
    q = h_ref.shape[1]
    funcs = turned_ref.shape[1]
    branches, sensor_count, width = w_ref.shape
    dims, hidden = w1_ref.shape
    cut = sensor_count // chunks
    scale = width ** (-0.5)
    at_once = h_ref.shape[0]
    ahead = at_once == chunks
    parts = [(k, c) for k in range(branches) for c in range(0, sensor_count, 2 * q)]
    copies = fetch(
        sems, 0, *[(w_hbm.at[k, pl.ds(c, 2 * q)], w_ref.at[k, pl.ds(c, 2 * q)]) for k, c in parts], (w2_hbm, w2_ref)
    )

    pre = [bias_ref[k : k + 1, :] for k in range(branches)]

    def sensors(i):
        return turned_ref[i // 2, :, i % 2 * q : (i % 2 + 1) * q]

    def multiply(i):
        k, c = parts[i]
        copies[i].wait()
        pre[k] = pre[k] + dot(turned_ref[i, :, : 2 * q], w_ref[k, c : c + 2 * q])

    done = 0
    first = first_layer(w1_ref, b1_ref)

    def coords(block):
        return jnp.concatenate([line_of(block, row + d, q) for d in range(dims)], axis=0)

    def units(j):
        h_ref[j] = hidden_units(coords(got_ref[j].astype(F32)), first)

    held = 1 if ahead else 0
    if ahead:
        for j in range(chunks - held):
            units(j)
            ready = len(parts) * max(j - 1, 0) // chunks
            while done < ready:
                multiply(done)
                done += 1
    for i in range(done, len(parts)):
        multiply(i)
    for j in range(chunks - held, chunks if ahead else 0):
        units(j)
    lats = [jnp.tanh(p).astype(BF).astype(F32) for p in pre]
    product = (lats[0] * lats[1] * lats[2]).astype(BF)
    offset = jnp.sum(product.astype(F32) * b2_ref[...], axis=1, keepdims=True)
    copies[-1].wait()
    mixed_full = dot(product, w2_ref[...], ((1,), (1,)))
    mixed = jnp.concatenate(pieces(mixed_full, 2), axis=0)

    place = lax.broadcasted_iota(jnp.int32, (funcs, q), 0).astype(F32)
    one = jnp.ones((), BF)
    g_ref[...] = jnp.zeros_like(g_ref)
    m_ref[...] = jnp.zeros_like(m_ref)
    r_ref[...] = jnp.zeros_like(r_ref)

    def residuals(j, slot):
        block = got_ref[j].astype(F32)
        xyz = coords(block)
        owner = line_of(block, row + dims, q)
        target = [
            block[c % rows : c % rows + 1, 2 * q + c // rows * LANES : 2 * q + (c // rows + 1) * LANES]
            for c in range(2 * q // LANES)
        ]
        target = jnp.concatenate(target, axis=1)
        target = target[:, :q] + target[:, q:]
        if not ahead:
            h_ref[slot] = hidden_units(xyz, first)
        scores = dot(mixed, h_ref[slot], ((1,), (1,)))
        scores = scores[:funcs] + scores[funcs:] + offset
        owned = (owner == place).astype(F32)
        pred = jnp.sum(owned * scores, axis=0, keepdims=True) * scale
        resid = (pred - target) / total_funcs
        coef = owned * (resid * scale)
        spread = jnp.concatenate([coef] + [coef * xyz[d : d + 1] for d in range(dims)], axis=0)
        coef_ref[slot] = jnp.concatenate(pieces(coef, 2) + pieces(spread, 2), axis=0)
        return coef

    def batch(start):
        r = r_ref[...]
        for slot in range(at_once):
            r = r + residuals(start + slot, slot)
        r_ref[...] = r
        g, m = g_ref[...], m_ref[...]
        for slot in range(at_once):
            h = h_ref[slot]
            g = g + dot(coef_ref[slot, : 2 * funcs], h)
            m = m + dot(coef_ref[slot, 2 * funcs :], (one - h) * (one + h))
        g_ref[...] = g
        m_ref[...] = m

    if ahead:
        batch(0)
    else:
        lax.fori_loop(0, chunks // at_once, lambda i, carry: (batch(i * at_once), carry)[1], 0)

    r = jnp.broadcast_to(jnp.sum(r_ref[...], axis=1, keepdims=True), (funcs, LANES))
    high, low = pieces(r, 2)
    lane = lax.broadcasted_iota(jnp.int32, r.shape, 1)
    r = jnp.where(lane < LANES // 2, high.astype(F32), low.astype(F32))
    half = (dims + 1) * funcs
    moments = m_ref[:half] + m_ref[half:]
    extra = up(-(-(dims + 1) * hidden // funcs), LANES)
    grads = []
    for d in range(dims + 1):
        grad = jnp.sum(moments[d * funcs : (d + 1) * funcs] * mixed_full, axis=0, keepdims=True)
        grads += [grad[:, c : c + extra] for c in range(0, hidden, extra)]
    me = lax.axis_index("query")
    columns = []
    for k in range(branches):
        mine = jnp.zeros((funcs, cut), F32)
        for j in range(chunks):
            line, at = divmod(k * sensor_count + j * cut, q)
            mine = jnp.where(me == j, sensors(line)[:, at : at + cut].astype(F32), mine)
        columns.append(mine)
    flat = out_ref.shape[1] - width - LANES - extra - branches * width
    if flat > branches * cut:
        columns.append(jnp.zeros((funcs, flat - branches * cut), F32))
    sums = [g_ref[:funcs] + g_ref[funcs:], r, stack(grads, funcs)]
    out_ref[...] = jnp.concatenate(sums + lats + columns, axis=1).astype(BF)


def tail_kernel(groups, early_width, *refs):
    w2_ref, b2_ref = refs[groups : groups + 2]
    outs, bufs, sems = refs[groups + 2 : groups + 8], refs[groups + 8 : groups + 14], refs[-1]
    gbw_ref, gbb_ref, gw1_ref, gb1_ref, gw2_ref, gb2_ref = bufs
    width = w2_ref.shape[1]
    branches, cut, _ = gbw_ref.shape
    dims = gw1_ref.shape[0]
    all_rows = [x[...].astype(F32) for x in refs[:groups]]
    ends = all_rows[0].shape[1] - early_width
    copies = []

    def send(index, *at):
        source, target = bufs[index], outs[index]
        if at:
            source, target = source.at[at], target.at[at]
        copies.extend(fetch(sems, len(copies), (source, target)))

    def columns(first, count):
        return jnp.concatenate([x[:, first : first + count] for x in all_rows], axis=0)

    lat = [columns(ends + k * width, width) for k in range(branches)]
    product = (lat[0] * lat[1] * lat[2]).astype(BF)
    g = columns(0, width).astype(BF)
    height = gw2_ref.shape[0] // BLOCKS
    for c in range(0, gw2_ref.shape[0], height):
        gw2_ref[c : c + height] = dot(g[:, c : c + height], product, ((0,), (0,)))
        send(4, pl.ds(c, height))
    r = columns(width, LANES)
    r = r[:, :1] + r[:, LANES // 2 : LANES // 2 + 1]
    dprod = dot(g, w2_ref[...]) + r * b2_ref[...]
    lines = columns(ends + branches * width, branches * cut)
    gbb = []
    for k in range(branches):
        others = [lat[j] for j in range(branches) if j != k]
        delta = (dprod * (others[0] * others[1] * (1.0 - lat[k] * lat[k]))).astype(BF)
        gbw_ref[k] = dot(lines[:, k * cut : (k + 1) * cut].astype(BF), delta, ((0,), (0,)))
        send(0, k)
        gbb.append(jnp.sum(delta.astype(F32), axis=0, keepdims=True))
    gbb_ref[...] = jnp.concatenate(gbb, axis=0)
    parts = all_rows[0][:, width + LANES : ends]
    for x in all_rows[1:]:
        parts = parts + x[:, width + LANES : ends]
    each = gw1_ref.shape[1] // parts.shape[1]
    grads = [
        jnp.concatenate([parts[d * each + c : d * each + c + 1] for c in range(each)], axis=1) for d in range(dims + 1)
    ]
    gb1_ref[...] = grads[0]
    gw1_ref[...] = jnp.concatenate(grads[1:], axis=0)
    gb2_ref[...] = jnp.sum(r * product.astype(F32), axis=0, keepdims=True)
    for index in (1, 2, 3, 5):
        send(index)
    wait(copies)


def shards(
    sensors, branch_w, branch_b, coords, func_index, targets, trunk_w1, trunk_b1, trunk_w2, trunk_b2
):
    branches, func_dev, sensor_count = sensors.shape
    dims, queries = coords.shape
    hidden, width = trunk_w2.shape
    nb, nq = lax.axis_size("branch"), lax.axis_size("query")
    assert func_dev == 1 and hidden == width and sensor_count % (2 * queries) == 0 and queries % (sensor_count // nq) == 0
    funcs = nq
    cut = sensor_count // nq
    row, rows, packed_width = plan(branches, sensor_count, dims, queries)
    at_once = nq if nq * queries * hidden * 2 <= 16 * MIB else 8
    assert nq % at_once == 0

    small = (branch_b, trunk_b2[None], trunk_w1, trunk_b1[None])
    packed, *small_here = pl.pallas_call(
        pack_kernel,
        out_shape=(
            jax.ShapeDtypeStruct((nq, rows, packed_width), BF),
            *[jax.ShapeDtypeStruct(x.shape, x.dtype) for x in small],
        ),
        in_specs=[HBM] * (4 + len(small)),
        out_specs=(VMEM,) * (1 + len(small)),
        scratch_shapes=[
            pltpu.VMEM((branches, sensor_count), BF),
            pltpu.VMEM((dims, queries), BF),
            pltpu.VMEM((1, queries), jnp.int32),
            pltpu.VMEM((1, queries), F32),
            pltpu.SemaphoreType.DMA((4 + len(small),)),
        ],
        compiler_params=pltpu.CompilerParams(vmem_limit_bytes=8 * MIB),
        name="pack",
    )(*in_hbm(sensors.reshape(branches, sensor_count), coords, func_index[None], targets[None], *small))
    got = lax.all_to_all(packed, "query", 0, 0, tiled=True)

    early_width = branches * width + up(branches * cut, LANES)
    sums_width = width + LANES + up(-(-(dims + 1) * hidden // funcs), LANES)
    sums, w2_here = pl.pallas_call(
        functools.partial(group_kernel, row, nb * nq),
        out_shape=(
            jax.ShapeDtypeStruct((funcs, sums_width + early_width), BF),
            jax.ShapeDtypeStruct((hidden, width), BF),
        ),
        in_specs=[VMEM] * 6 + [HBM] * 2,
        out_specs=(VMEM,) * 2,
        scratch_shapes=[
            pltpu.VMEM((at_once, queries, hidden), BF),
            pltpu.VMEM(branch_w.shape, BF),
            pltpu.VMEM((2 * funcs, hidden), F32),
            pltpu.VMEM((2 * (dims + 1) * funcs, hidden), F32),
            pltpu.VMEM((funcs, queries), F32),
            pltpu.VMEM((at_once, 2 * (dims + 2) * funcs, queries), BF),
            pltpu.SemaphoreType.DMA((row // 2 + 1,)),
        ],
        compiler_params=pltpu.CompilerParams(vmem_limit_bytes=40 * MIB),
        cost_estimate=pl.CostEstimate(
            flops=2 * 1024 * nq * queries * hidden, bytes_accessed=2 * branch_w.size, transcendentals=0
        ),
        name="group",
    )(got, got.transpose(1, 0, 2), *small_here, *in_hbm(branch_w, trunk_w2))

    def shift(x, k):
        return lax.ppermute(x, "branch", [(i, (i + k) % nb) for i in range(nb)])

    def swap(x):
        return lax.ppermute(x, "branch", [(i, i ^ 1) for i in range(nb)])

    if nb % 2:
        every = [sums] + [shift(sums, k) for k in range(1, nb)]
    else:
        every = [sums] + [shift(sums, k) for k in range(2, nb, 2)]
        every += [swap(x) for x in every]
    outs = (
        jax.ShapeDtypeStruct((branches, cut, width), F32),
        jax.ShapeDtypeStruct((branches, width), F32),
        jax.ShapeDtypeStruct((dims, hidden), F32),
        jax.ShapeDtypeStruct((1, hidden), F32),
        jax.ShapeDtypeStruct((hidden, width), F32),
        jax.ShapeDtypeStruct((1, width), F32),
    )
    gbw, gbb, gw1, gb1, gw2, gb2 = pl.pallas_call(
        functools.partial(tail_kernel, nb, early_width),
        out_shape=outs,
        in_specs=[VMEM] * (nb + 2),
        out_specs=(HBM,) * len(outs),
        scratch_shapes=[pltpu.VMEM(x.shape, F32) for x in outs]
        + [pltpu.SemaphoreType.DMA((BLOCKS + branches + 4,))],
        compiler_params=pltpu.CompilerParams(vmem_limit_bytes=24 * MIB),
        name="tail",
    )(*every, w2_here, small_here[1])
    return (gbw, gbb, gw1, gb1[0], gw2, gb2[0])


def solution(mesh):
    placed = (
        P(None, ("branch", "query"), None),
        P(),
        P(),
        P(None, ("branch", "query")),
        P(("branch", "query")),
        P(("branch", "query")),
        P(),
        P(),
        P(),
        P(),
    )
    return jax.shard_map(
        shards,
        mesh=mesh,
        in_specs=placed,
        out_specs=(P(None, "query", None), P(), P(), P(), P(), P()),
        check_vma=False,
    )
```
